32 devices in a mesh: grp: 2 (over y), res: 8 (over z, x), ta: 2 (over core).
Axes of the slice: x: 2, y: 2, z: 4, core: 2. Of those that a mesh axis runs over, the one named last changes fastest.
Arguments:
- log_order: int32 [8, 512], P('res'), may hold values from 1 to 4096, as said below
- t_start: int32 [2], P('grp'), parts along dimension 0, may hold values from 160 to 319
- term_counts: int32 [1024], P(('grp', 'ta')), parts along dimension 0, may hold values from 4 to 32, as said below
Outputs:
- refined: float32 [2, 8, 512, 2048], P(None, None, 'res', ('grp', 'ta')), parts along dimension 3
The draws below stay inside these ranges and needn't reach their ends.
There are 2 independent parts, one for each index of `grp`. The reference program is written for one: setup_inputs(seed, part) draws one part's arguments, and reference() takes and returns one part's arrays. A program takes and returns all parts, laid end to end along the dimension named above; an argument that names none is the same for every part. Nothing has to cross between parts.
Inputs may be any that keep to these rules, and one draw needn't show every extreme that they name: `log_order`: every residue 1 to 4096 appears once. `term_counts`: at least an eighth of t_m plus two, except at the first point.
All inputs are finite; a program needn't handle non-finite values.
Results may differ from the reference program's by a relative error of at most 0.00023.
Values sent between devices are 32-bit elements; how exact they have to be, the bound alone decides.
A program may use at most 64 MiB of HBM per device.

```python
import math
import jax
import jax.numpy as jnp
from jax import lax

RES_DEV = 512
T_DEV = 256
TAPS = 8
NMIN = 4
MAXN = 32
Q1 = 4096
QMOD = 4097
TPTS = 512
N_RES = 8
N_TA = 2


def draw_log_order(key, part):
    shuffled = jax.random.permutation(key, RES_DEV * N_RES) + 1
    return shuffled.reshape(N_RES, RES_DEV).astype(jnp.int32)


def start_index(key, part):
    drawn = jax.random.randint(jax.random.fold_in(key, 11), (), 160, 320).astype(jnp.int32)
    return jnp.where(part % 2 == 1, jnp.int32(319), drawn).astype(jnp.int32)


def draw_t_start(key, part):
    return start_index(key, part).reshape(1)


def draw_term_counts(key, part):
    first = start_index(key, part)
    points = T_DEV * N_TA
    extra = jax.random.randint(jax.random.fold_in(key, 7), (points,), 0, 5).astype(jnp.int32)
    lattice = first + jnp.arange(points, dtype=jnp.int32)
    values = (lattice + 127) // 128 + 2 + extra
    values = jnp.clip(values, NMIN, MAXN)
    values = values.at[0].set(NMIN).at[points - 1].set(MAXN)
    return values.astype(jnp.int32)


def setup_inputs(seed: int = 0, part: int = 0) -> dict:
    arg_keys = jax.random.split(jax.random.key(seed), 4)
    part_keys = jax.random.split(jax.random.fold_in(arg_keys[3], part), 4)
    log_order = draw_log_order(jax.random.fold_in(arg_keys[3], 71), part)
    t_start = draw_t_start(jax.random.fold_in(jax.random.fold_in(arg_keys[3], part), 71), part)
    term_counts = draw_term_counts(jax.random.fold_in(jax.random.fold_in(arg_keys[3], part), 71), part)
    return {"log_order": log_order, "t_start": t_start, "term_counts": term_counts}


time_step = 0.0625

def inverse_power(base_value, t_values):
    modulus = lax.rsqrt(base_value)
    phase_now = t_values * jnp.log(base_value)
    return (modulus * jnp.cos(phase_now), -modulus * jnp.sin(phase_now))

def hurwitz_values(x_values, t_values, count_row, most_terms):
    shape_out = (x_values.shape[0], t_values.shape[1])

    def add_term(term_index, running):
        sum_re, sum_im = running
        base_value = term_index.astype(x_values.dtype) + x_values
        piece_re, piece_im = inverse_power(base_value, t_values)
        active = term_index < count_row
        return (sum_re + jnp.where(active, piece_re, 0.0), sum_im + jnp.where(active, piece_im, 0.0))
    zeros_init = jnp.zeros(shape_out, x_values.dtype)
    sum_re, sum_im = lax.fori_loop(0, most_terms, add_term, (zeros_init, zeros_init))
    tail_base = count_row.astype(x_values.dtype) + x_values
    power_re, power_im = inverse_power(tail_base, t_values)
    denominator = 0.25 + t_values * t_values
    lifted_re = tail_base * power_re
    lifted_im = tail_base * power_im
    total_re = sum_re + (-0.5 * lifted_re + t_values * lifted_im) / denominator + 0.5 * power_re
    total_im = sum_im + (-t_values * lifted_re - 0.5 * lifted_im) / denominator + 0.5 * power_im
    total_re = total_re + (0.5 * power_re - t_values * power_im) / (12.0 * tail_base)
    total_im = total_im + (0.5 * power_im + t_values * power_re) / (12.0 * tail_base)
    cubic_re = 1.875 - 4.5 * t_values * t_values
    cubic_im = 5.75 * t_values - t_values * t_values * t_values
    cube_base = 720.0 * tail_base * tail_base * tail_base
    total_re = total_re - (cubic_re * power_re - cubic_im * power_im) / cube_base
    total_im = total_im - (cubic_re * power_im + cubic_im * power_re) / cube_base
    return (total_re, total_im)

def sinc_value(offset):
    return math.sin(math.pi * offset) / (math.pi * offset)

def refine(padded, half_width, length):
    coarse = padded[..., half_width:half_width + length]
    middle = jnp.zeros_like(coarse)
    for offset in range(1 - half_width, half_width + 1):
        weight = sinc_value(offset - 0.5) * sinc_value((offset - 0.5) / half_width)
        middle = middle + weight * padded[..., half_width + offset:half_width + offset + length]
    stacked = jnp.stack([coarse, middle], axis=-1)
    return stacked.reshape(stacked.shape[:-2] + (2 * length,))

def reference(log_order, t_start, term_counts):
    positions = jnp.arange(TPTS, dtype=jnp.int32)
    t_values = ((t_start[0] + positions).astype(jnp.float32) * time_step)[None, :]
    order_flat = jnp.transpose(log_order).reshape(-1)
    x_values = (order_flat.astype(jnp.float32) / jnp.float32(QMOD))[:, None]
    zeta_re, zeta_im = hurwitz_values(x_values, t_values, term_counts[None, :], MAXN)
    spectrum = jnp.fft.ifft(lax.complex(zeta_re, zeta_im), axis=0) * Q1
    spec_re = jnp.real(spectrum)
    spec_im = jnp.imag(spectrum)
    factor_re, factor_im = inverse_power(jnp.float32(QMOD), t_values)
    lval_re = spec_re * factor_re - spec_im * factor_im
    lval_im = spec_re * factor_im + spec_im * factor_re
    stacked = jnp.stack([lval_re, lval_im]).reshape(2, N_RES, RES_DEV, TPTS)
    padded = jnp.pad(stacked, ((0, 0), (0, 0), (0, 0), (TAPS, TAPS)))
    return refine(padded, TAPS, TPTS)
```

```python
import functools
import math

import jax
import jax.numpy as jnp
import ml_dtypes
import numpy as np
from jax import lax
from jax.experimental import pallas as pl
from jax.experimental.pallas import tpu as pltpu
from jax.sharding import PartitionSpec as P

TAPS = 8
MAXN = 32
LANES = 128
TILE = 8

SIN_COEFS = (
    6.2831854820251465, -41.34170150756836, 81.60513305664062, -76.7030029296875,
    42.02585220336914, -14.899578094482422, 3.2377800941467285,
)
COS_COEFS = (
    1.0, -19.73920440673828, 64.93911743164062, -85.45011138916016,
    60.16743087768555, -25.96688461303711, 6.527706146240234,
)
ROUNDER = 12582912.0


def sincos_turns(turns):
    frac = turns - ((turns + ROUNDER) - ROUNDER)
    square = frac * frac
    sin_acc = jnp.full_like(square, SIN_COEFS[-1])
    cos_acc = jnp.full_like(square, COS_COEFS[-1])
    for sin_c, cos_c in zip(SIN_COEFS[-2::-1], COS_COEFS[-2::-1]):
        sin_acc = sin_acc * square + sin_c
        cos_acc = cos_acc * square + cos_c
    return sin_acc * frac, cos_acc


def split_bf16(values):
    high = values.astype(jnp.bfloat16)
    return high, (values - high.astype(jnp.float32)).astype(jnp.bfloat16)


def split_const(values):
    high = values.astype(np.float32).astype(ml_dtypes.bfloat16)
    low = (values - high.astype(np.float64)).astype(np.float32).astype(ml_dtypes.bfloat16)
    return high, low


def dot_nt(left, right):
    return lax.dot_general(
        left, right, (((1,), (1,)), ((), ())), preferred_element_type=jnp.float32
    )


def dot_nn(left, right):
    return jnp.dot(left, right, preferred_element_type=jnp.float32)


def fourier_table(rows):
    ids = np.arange(rows)
    phase = 2.0 * np.pi * (np.outer(ids, ids) % rows) / rows
    return np.stack(split_const(np.cos(phase)) + split_const(np.sin(phase)))


def sinc_value(offset):
    return math.sin(math.pi * offset) / (math.pi * offset)


def tap_weight(offset):
    return sinc_value(offset - 0.5) * sinc_value((offset - 0.5) / TAPS)


def refine_table(length):
    table = np.zeros((length, 2 * length))
    for m in range(length):
        table[m, 2 * m] = 1.0
        for offset in range(1 - TAPS, TAPS + 1):
            if 0 <= m + offset < length:
                table[m + offset, 2 * m + 1] = tap_weight(offset)
    return np.stack(split_const(table))


def edge_table(length, slabs):
    side = np.zeros((2, TILE, LANES))
    for h in range(TAPS):
        for column in range(LANES):
            if column % 2 == 0:
                continue
            m = (2 * length - LANES + column) // 2
            offset = length + h - m
            if 1 - TAPS <= offset <= TAPS:
                side[0, h, column] = tap_weight(offset)
            m = column // 2
            offset = h - TAPS - m
            if 1 - TAPS <= offset <= TAPS:
                side[1, h, column] = tap_weight(offset)
    full = np.zeros((2, slabs * TILE, slabs * LANES))
    for slab in range(slabs):
        full[:, slab * TILE : (slab + 1) * TILE, slab * LANES : (slab + 1) * LANES] = side
    high, low = split_const(full)
    return np.stack([high, low], axis=1)


class Shape:
    def __init__(self, rows, slabs, length):
        self.rows = rows
        self.slabs = slabs
        self.length = length
        self.block = rows // slabs
        self.tiles = length // TILE + 1
        self.halves = length // LANES


def prepare(shape, order_ref, turn_re, turn_im, wave_re, wave_im, base_t):
    rows = shape.rows
    modulus = float(shape.slabs * rows + 1)
    order_row = order_ref[...].astype(jnp.float32)
    term = lax.broadcasted_iota(jnp.int32, (MAXN, rows), 0).astype(jnp.float32)
    base = term * modulus + order_row
    log_turn = jnp.log(base) * (1.0 / (2.0 * math.pi))
    amp = lax.rsqrt(base)
    step_sin, step_cos = sincos_turns(log_turn * (TILE / 16.0))
    offsets = lax.broadcasted_iota(jnp.int32, (TILE, rows), 0).astype(jnp.float32)
    t_first = (base_t + offsets) * 0.0625
    for n in range(MAXN):
        sin, cos = sincos_turns(t_first * log_turn[n : n + 1, :])
        amp_row = amp[n : n + 1, :]
        wave_re[n] = amp_row * cos
        wave_im[n] = -amp_row * sin
        turn_re[n] = jnp.broadcast_to(step_cos[n : n + 1, :], (TILE, rows))
        turn_im[n] = jnp.broadcast_to(-step_sin[n : n + 1, :], (TILE, rows))


def sum_tiles(shape, first, count, order_ref, counts, turn_re, turn_im, wave_re, wave_im, zeta_re, zeta_im, base_t):
    modulus = float(shape.slabs * shape.rows + 1)
    row0 = first * TILE

    def lane_block(block, carry):
        lanes = pl.ds(pl.multiple_of(block * LANES, LANES), LANES)
        limits = [counts[row0 + a * TILE : row0 + (a + 1) * TILE, :] for a in range(count)]

        def term(n, sums):
            now_re = wave_re[n, :, lanes]
            now_im = wave_im[n, :, lanes]
            rot_re = turn_re[n, :, lanes]
            rot_im = turn_im[n, :, lanes]
            n_float = lax.convert_element_type(n, jnp.float32)
            out = []
            for a in range(count):
                active = limits[a] > n_float
                out.append(sums[2 * a] + jnp.where(active, now_re, 0.0))
                out.append(sums[2 * a + 1] + jnp.where(active, now_im, 0.0))
                now_re, now_im = (
                    now_re * rot_re - now_im * rot_im,
                    now_re * rot_im + now_im * rot_re,
                )
            wave_re[n, :, lanes] = now_re
            wave_im[n, :, lanes] = now_im
            return tuple(out)

        zero = jnp.zeros((TILE, LANES), jnp.float32)
        sums = lax.fori_loop(0, MAXN, term, (zero,) * (2 * count))
        residue = jnp.broadcast_to(order_ref[:, lanes].astype(jnp.float32), (TILE, LANES))
        fraction = residue * (1.0 / modulus)
        offsets = lax.broadcasted_iota(jnp.int32, (TILE, LANES), 0).astype(jnp.float32)
        for a in range(count):
            limit = limits[a]
            t_now = (base_t + float(row0 + a * TILE) + offsets) * 0.0625
            t_square = t_now * t_now
            inverse_den = 1.0 / (0.25 + t_square)
            cubic_re = 1.875 - 4.5 * t_square
            cubic_im = t_now * (5.75 - t_square)
            whole_base = limit * modulus + residue
            tail_base = limit + fraction
            inverse = 1.0 / tail_base
            cube = inverse * inverse * inverse * (1.0 / 720.0)
            twelfth = inverse * (1.0 / 12.0)
            lifted = tail_base * inverse_den
            gain_re = 0.5 + 0.5 * twelfth - 0.5 * lifted - cubic_re * cube
            gain_im = t_now * (twelfth - lifted) - cubic_im * cube
            sin, cos = sincos_turns(t_now * (jnp.log(whole_base) * (1.0 / (2.0 * math.pi))))
            amp = lax.rsqrt(whole_base)
            power_re = amp * cos
            power_im = -amp * sin
            place = slice(row0 + a * TILE, row0 + (a + 1) * TILE)
            zeta_re[place, lanes] = sums[2 * a] + (gain_re * power_re - gain_im * power_im)
            zeta_im[place, lanes] = sums[2 * a + 1] + (gain_re * power_im + gain_im * power_re)
        return carry

    lax.fori_loop(0, shape.rows // LANES, lane_block, 0)


def make_twist(shape, slab_index, twist_cos, twist_sin):
    ids = lax.broadcasted_iota(jnp.int32, (shape.rows, LANES), 0)
    turns = (ids * slab_index).astype(jnp.float32) * (1.0 / (shape.slabs * shape.rows))
    sin, cos = sincos_turns(turns)
    twist_cos[...] = cos
    twist_sin[...] = sin


def transform_half(shape, half, skip, zeta_re, zeta_im, tables, twist_cos, twist_sin, store):
    place = pl.ds(pl.multiple_of(half * LANES + skip, TILE), LANES)
    both = jnp.concatenate([zeta_re[place, :], zeta_im[place, :]], axis=0)
    high, low = split_bf16(both)
    chunk = 2 * shape.block
    for piece in range(shape.rows // chunk):
        rows = slice(piece * chunk, (piece + 1) * chunk)
        cos_high = tables[0, rows, :]
        sin_high = tables[2, rows, :]
        with_cos = dot_nt(cos_high, high) + dot_nt(cos_high, low) + dot_nt(tables[1, rows, :], high)
        with_sin = dot_nt(sin_high, high) + dot_nt(sin_high, low) + dot_nt(tables[3, rows, :], high)
        mixed_re = with_cos[:, :LANES] - with_sin[:, LANES:]
        mixed_im = with_sin[:, :LANES] + with_cos[:, LANES:]
        t_cos = twist_cos[rows, :]
        t_sin = twist_sin[rows, :]
        out_re = t_cos * mixed_re - t_sin * mixed_im
        out_im = t_sin * mixed_re + t_cos * mixed_im
        for sub in range(2):
            cut = slice(sub * shape.block, (sub + 1) * shape.block)
            store(2 * piece + sub, 0, out_re[cut])
            store(2 * piece + sub, 1, out_im[cut])


def transform_edge(shape, place, slab_index, zeta_re, zeta_im, tables, store):
    both = jnp.concatenate([zeta_re[place, :], zeta_im[place, :]], axis=0)
    high, low = split_bf16(both)
    with_cos = dot_nn(high, tables[0]) + dot_nn(low, tables[0]) + dot_nn(high, tables[1])
    with_sin = dot_nn(high, tables[2]) + dot_nn(low, tables[2]) + dot_nn(high, tables[3])
    mixed_re = with_cos[:TILE] - with_sin[TILE:]
    mixed_im = with_sin[:TILE] + with_cos[TILE:]
    ids = lax.broadcasted_iota(jnp.int32, (TILE, shape.rows), 1)
    sin, cos = sincos_turns(
        (ids * slab_index).astype(jnp.float32) * (1.0 / (shape.slabs * shape.rows))
    )
    out_re = cos * mixed_re - sin * mixed_im
    out_im = sin * mixed_re + cos * mixed_im
    lane = lax.broadcasted_iota(jnp.int32, (TILE, LANES), 1)
    for pair in range(shape.slabs // 2):
        cut = slice(pair * LANES, (pair + 1) * LANES)
        part_re = out_re[:, cut]
        part_im = out_im[:, cut]
        store(2 * pair, jnp.where(lane < LANES // 2, part_re, pltpu.roll(part_im, LANES // 2, 1)))
        store(
            2 * pair + 1,
            jnp.where(lane < LANES // 2, pltpu.roll(part_re, LANES // 2, 1), part_im),
        )


def column_counts(shape, counts_row, counts):
    width = counts.shape[0]
    row = jnp.broadcast_to(counts_row.astype(jnp.float32), (LANES, width))
    for cut in range(width // LANES):
        part = row[:, cut * LANES : (cut + 1) * LANES]
        counts[cut * LANES : (cut + 1) * LANES, :] = part.T


def zeta_kernel(shape, start_ref, order_ref, count_ref, tables, main_ref, edge_ref,
                turn_re, turn_im, wave_re, wave_im, zeta_re, zeta_im, counts, twist_cos, twist_sin):
    slab_index = lax.axis_index("res")
    ta_index = lax.axis_index("ta")
    skip = ta_index * TILE
    base_t = (start_ref[0] + ta_index * (shape.length - TILE)).astype(jnp.float32)
    column_counts(shape, count_ref[...], counts)
    make_twist(shape, slab_index, twist_cos, twist_sin)
    prepare(shape, order_ref, turn_re, turn_im, wave_re, wave_im, base_t)
    first = 0
    for half in range(shape.halves):
        for count in ((9, 8) if half == 0 else (8, 8)):
            sum_tiles(shape, first, count, order_ref, counts, turn_re, turn_im, wave_re, wave_im,
                      zeta_re, zeta_im, base_t)
            first += count

        def store(block, part, values, half=half):
            main_ref[half, block, part] = values

        transform_half(shape, half, skip, zeta_re, zeta_im, tables, twist_cos, twist_sin, store)

    def store_edge(block, values):
        edge_ref[block] = values

    edge_place = pl.ds(pl.multiple_of((1 - ta_index) * shape.length, TILE), TILE)
    transform_edge(shape, edge_place, slab_index, zeta_re, zeta_im, tables, store_edge)


def turn_eighth(re, im, eighths):
    root = math.sqrt(0.5)
    if eighths == 0:
        return re, im
    if eighths == 1:
        return root * (re - im), root * (re + im)
    if eighths == 2:
        return -im, re
    return -root * (re + im), root * (re - im)


def fft_eight(parts):
    def step(values):
        size = len(values)
        if size == 1:
            return values
        even = step(values[0::2])
        odd = step(values[1::2])
        low, high = [], []
        for k in range(size // 2):
            o_re, o_im = turn_eighth(*odd[k], k * (8 // size))
            e_re, e_im = even[k]
            low.append((e_re + o_re, e_im + o_im))
            high.append((e_re - o_re, e_im - o_im))
        return low + high

    return step(parts)


def refine_kernel(shape, chunk, main_ref, edge_ref, table, edge_tab, out_ref, edge_out):
    step = pl.program_id(0)
    slabs = shape.slabs
    half_lanes = LANES // 2
    ta_index = lax.axis_index("ta")

    @pl.when(step == 0)
    def _():
        lane = lax.broadcasted_iota(jnp.int32, (TILE, LANES), 1)
        parts = [(edge_ref[p], pltpu.roll(edge_ref[p], half_lanes, 1)) for p in range(slabs)]
        mixed = fft_eight(parts)
        rows = [jnp.where(lane < half_lanes, re, pltpu.roll(im, half_lanes, 1)) for re, im in mixed]
        stacked = jnp.concatenate(rows + rows, axis=0)
        high, low = split_bf16(stacked.T[:, : slabs * TILE])
        tab_high = edge_tab[ta_index, 0]
        tab_low = edge_tab[ta_index, 1]
        edge_out[...] = dot_nn(high, tab_high) + dot_nn(low, tab_high) + dot_nn(high, tab_low)

    parts = []
    for p in range(slabs):
        re = jnp.concatenate([main_ref[h, p, 0] for h in range(shape.halves)], axis=1)
        im = jnp.concatenate([main_ref[h, p, 1] for h in range(shape.halves)], axis=1)
        parts.append((re, im))
    mixed = fft_eight(parts)
    stacked = jnp.concatenate([m[0] for m in mixed] + [m[1] for m in mixed], axis=0)
    high, low = split_bf16(stacked)
    result = dot_nn(high, table[0]) + dot_nn(low, table[0]) + dot_nn(high, table[1])
    edge_lanes = pl.ds(
        pl.multiple_of((1 - ta_index) * (2 * shape.length - LANES), LANES), LANES
    )
    for part in range(2):
        rows = pl.ds(pl.multiple_of(part * shape.block + step * chunk, TILE), chunk)
        for w in range(slabs):
            at = (part * slabs + w) * chunk
            out_ref[part, w] = result[at : at + chunk]
            out_ref[part, w, :, edge_lanes] += edge_out[rows, w * LANES : (w + 1) * LANES]


def fast_device(log_order, t_start, term_counts):
    shape = Shape(log_order.shape[1], lax.axis_size("res"), term_counts.shape[0])
    rows, slabs, length = shape.rows, shape.slabs, shape.length
    ta_index = lax.axis_index("ta")
    other = lax.ppermute(term_counts, "ta", [(0, 1), (1, 0)])
    pad = jnp.full((LANES - TILE,), MAXN, jnp.int32)
    counts = jnp.where(
        ta_index == 0,
        jnp.concatenate([term_counts, other[:TILE], pad]),
        jnp.concatenate([other[length - TILE :], term_counts, pad]),
    )
    f32 = jnp.float32
    vmem = pl.BlockSpec(memory_space=pltpu.VMEM)
    main, edge = pl.pallas_call(
        functools.partial(zeta_kernel, shape),
        out_shape=(
            jax.ShapeDtypeStruct((shape.halves, slabs, 2, shape.block, LANES), f32),
            jax.ShapeDtypeStruct((slabs, TILE, LANES), f32),
        ),
        in_specs=[pl.BlockSpec(memory_space=pltpu.SMEM), vmem, vmem, vmem],
        out_specs=(vmem, vmem),
        scratch_shapes=[
            pltpu.VMEM((MAXN, TILE, rows), f32),
            pltpu.VMEM((MAXN, TILE, rows), f32),
            pltpu.VMEM((MAXN, TILE, rows), f32),
            pltpu.VMEM((MAXN, TILE, rows), f32),
            pltpu.VMEM((length + TILE, rows), f32),
            pltpu.VMEM((length + TILE, rows), f32),
            pltpu.VMEM((length + LANES, LANES), f32),
            pltpu.VMEM((rows, LANES), f32),
            pltpu.VMEM((rows, LANES), f32),
        ],
        compiler_params=pltpu.CompilerParams(vmem_limit_bytes=48 * 2**20),
    )(t_start, log_order, counts[None, :], jnp.asarray(fourier_table(rows)))
    main = lax.all_to_all(main, "res", split_axis=1, concat_axis=1, tiled=True)
    edge = lax.all_to_all(edge, "res", split_axis=0, concat_axis=0, tiled=True)
    return refine_call(shape, main, edge)


def refine_call(shape, main, edge):
    slabs, length = shape.slabs, shape.length
    chunk = 16
    f32 = jnp.float32
    return pl.pallas_call(
        functools.partial(refine_kernel, shape, chunk),
        grid=(shape.block // chunk,),
        out_shape=jax.ShapeDtypeStruct((2, slabs, shape.block, 2 * length), f32),
        in_specs=[
            pl.BlockSpec((shape.halves, slabs, 2, chunk, LANES), lambda i: (0, 0, 0, i, 0)),
            pl.BlockSpec((slabs, TILE, LANES), lambda i: (0, 0, 0)),
            pl.BlockSpec((2, length, 2 * length), lambda i: (0, 0, 0)),
            pl.BlockSpec((2, 2, slabs * TILE, slabs * LANES), lambda i: (0, 0, 0, 0)),
        ],
        out_specs=pl.BlockSpec((2, slabs, chunk, 2 * length), lambda i: (0, 0, i, 0)),
        scratch_shapes=[pltpu.VMEM((LANES, slabs * LANES), f32)],
        compiler_params=pltpu.CompilerParams(vmem_limit_bytes=48 * 2**20),
    )(main, edge, jnp.asarray(refine_table(length)), jnp.asarray(edge_table(length, slabs)))


time_step = 0.0625


def padded_2(block, sides, width):
    for axis, dim in sides:
        count = lax.axis_size(axis)
        forward = [(i, i + 1) for i in range(count - 1)]
        backward = [(target, source) for source, target in forward]
        low = lax.ppermute(
            lax.slice_in_dim(block, block.shape[dim] - width, None, axis=dim), axis, forward
        )
        high = lax.ppermute(lax.slice_in_dim(block, 0, width, axis=dim), axis, backward)
        block = jnp.concatenate([low, block, high], axis=dim)
    return block


def inverse_power(base_value, t_values):
    modulus = lax.rsqrt(base_value)
    phase_now = t_values * jnp.log(base_value)
    return (modulus * jnp.cos(phase_now), -modulus * jnp.sin(phase_now))


def hurwitz_values(x_values, t_values, count_row, most_terms):
    shape_out = (x_values.shape[0], t_values.shape[1])

    def add_term(term_index, running):
        sum_re, sum_im = running
        base_value = term_index.astype(x_values.dtype) + x_values
        piece_re, piece_im = inverse_power(base_value, t_values)
        active = term_index < count_row
        return (
            sum_re + jnp.where(active, piece_re, 0.0),
            sum_im + jnp.where(active, piece_im, 0.0),
        )

    zeros_init = jnp.zeros(shape_out, x_values.dtype)
    sum_re, sum_im = lax.fori_loop(0, most_terms, add_term, (zeros_init, zeros_init))
    tail_base = count_row.astype(x_values.dtype) + x_values
    power_re, power_im = inverse_power(tail_base, t_values)
    denominator = 0.25 + t_values * t_values
    lifted_re = tail_base * power_re
    lifted_im = tail_base * power_im
    total_re = sum_re + (-0.5 * lifted_re + t_values * lifted_im) / denominator + 0.5 * power_re
    total_im = sum_im + (-t_values * lifted_re - 0.5 * lifted_im) / denominator + 0.5 * power_im
    total_re = total_re + (0.5 * power_re - t_values * power_im) / (12.0 * tail_base)
    total_im = total_im + (0.5 * power_im + t_values * power_re) / (12.0 * tail_base)
    cubic_re = 1.875 - 4.5 * t_values * t_values
    cubic_im = 5.75 * t_values - t_values * t_values * t_values
    cube_base = 720.0 * tail_base * tail_base * tail_base
    total_re = total_re - (cubic_re * power_re - cubic_im * power_im) / cube_base
    total_im = total_im - (cubic_re * power_im + cubic_im * power_re) / cube_base
    return (total_re, total_im)


def refine(padded, half_width, length):
    coarse = padded[..., half_width : half_width + length]
    middle = jnp.zeros_like(coarse)
    for offset in range(1 - half_width, half_width + 1):
        weight = sinc_value(offset - 0.5) * sinc_value((offset - 0.5) / half_width)
        middle = middle + weight * padded[..., half_width + offset : half_width + offset + length]
    stacked = jnp.stack([coarse, middle], axis=-1)
    return stacked.reshape(stacked.shape[:-2] + (2 * length,))


def matmul_high(left, right):
    return jnp.dot(left, right, precision=lax.Precision.HIGHEST, preferred_element_type=jnp.float32)


def per_device(log_order, t_start, term_counts):
    rows_here = log_order.shape[1]
    slabs = lax.axis_size("res")
    slab_index = lax.axis_index("res")
    length_here = term_counts.shape[0]
    ta_index = lax.axis_index("ta")
    modulus_int = slabs * rows_here + 1
    x_values = log_order.reshape(rows_here, 1).astype(jnp.float32) / jnp.float32(modulus_int)
    row_ids = jnp.arange(rows_here, dtype=jnp.int32)
    first_phase = (row_ids[:, None] * row_ids[None, :] % rows_here).astype(jnp.float32) * (
        2.0 * math.pi / rows_here
    )
    first_cos = jnp.cos(first_phase)
    first_sin = jnp.sin(first_phase)
    twist_phase = (row_ids * slab_index).astype(jnp.float32)[:, None] * (
        2.0 * math.pi / (slabs * rows_here)
    )
    twist_cos = jnp.cos(twist_phase)
    twist_sin = jnp.sin(twist_phase)
    slab_ids = jnp.arange(slabs, dtype=jnp.int32)
    second_phase = (slab_ids[:, None] * slab_ids[None, :] % slabs).astype(jnp.float32) * (
        2.0 * math.pi / slabs
    )
    second_cos = jnp.cos(second_phase)
    second_sin = jnp.sin(second_phase)
    positions = ta_index * length_here + jnp.arange(length_here, dtype=jnp.int32)
    count_row = term_counts[None, :]
    t_values = ((t_start[0] + positions).astype(jnp.float32) * time_step)[None, :]
    zeta_re, zeta_im = hurwitz_values(x_values, t_values, count_row, MAXN)
    mixed_re = matmul_high(first_cos, zeta_re) - matmul_high(first_sin, zeta_im)
    mixed_im = matmul_high(first_sin, zeta_re) + matmul_high(first_cos, zeta_im)
    turned_re = twist_cos * mixed_re - twist_sin * mixed_im
    turned_im = twist_sin * mixed_re + twist_cos * mixed_im
    sectioned = jnp.stack([turned_re, turned_im])[:, None]
    block_in = lax.all_to_all(sectioned, "res", split_axis=2, concat_axis=1, tiled=True)
    part_re = block_in[0]
    part_im = block_in[1]

    def mix(table, values):
        return jnp.einsum(
            "wp,psn->wsn",
            table,
            values,
            precision=lax.Precision.HIGHEST,
            preferred_element_type=jnp.float32,
        )

    out_re = mix(second_cos, part_re) - mix(second_sin, part_im)
    out_im = mix(second_sin, part_re) + mix(second_cos, part_im)
    spectrum = jnp.stack([out_re, out_im])
    factor_re, factor_im = inverse_power(jnp.float32(modulus_int), t_values)
    lval_re = spectrum[0] * factor_re - spectrum[1] * factor_im
    lval_im = spectrum[0] * factor_im + spectrum[1] * factor_re
    lvals = jnp.stack([lval_re, lval_im])
    padded = padded_2(lvals, (("ta", 3),), TAPS)
    return refine(padded, TAPS, length_here)


def solution(mesh):
    placed = (P("res", None), P("grp"), P(("grp", "ta")))
    return jax.shard_map(
        fast_device if mesh.shape["res"] == 8 and mesh.shape["ta"] == 2 else per_device,
        mesh=mesh,
        in_specs=placed,
        out_specs=P(None, None, "res", ("grp", "ta")),
        check_vma=False,
    )
```

```python
import functools
import math

import jax
import jax.numpy as jnp
import ml_dtypes
import numpy as np
from jax import lax
from jax.experimental import pallas as pl
from jax.experimental.pallas import tpu as pltpu
from jax.sharding import PartitionSpec as P

TAPS = 8
MAXN = 32
LANES = 128
TILE = 8

SIN_COEFS = (
    6.2831854820251465, -41.34170150756836, 81.60513305664062, -76.7030029296875,
    42.02585220336914, -14.899578094482422, 3.2377800941467285,
)
COS_COEFS = (
    1.0, -19.73920440673828, 64.93911743164062, -85.45011138916016,
    60.16743087768555, -25.96688461303711, 6.527706146240234,
)
ROUNDER = 12582912.0


def sincos_turns(turns):
    frac = turns - ((turns + ROUNDER) - ROUNDER)
    square = frac * frac
    sin_acc = jnp.full_like(square, SIN_COEFS[-1])
    cos_acc = jnp.full_like(square, COS_COEFS[-1])
    for sin_c, cos_c in zip(SIN_COEFS[-2::-1], COS_COEFS[-2::-1]):
        sin_acc = sin_acc * square + sin_c
        cos_acc = cos_acc * square + cos_c
    return sin_acc * frac, cos_acc


def split_bf16(values):
    high = values.astype(jnp.bfloat16)
    return high, (values - high.astype(jnp.float32)).astype(jnp.bfloat16)


def split_const(values):
    high = values.astype(np.float32).astype(ml_dtypes.bfloat16)
    low = (values - high.astype(np.float64)).astype(np.float32).astype(ml_dtypes.bfloat16)
    return high, low


def dot_nt(left, right):
    return lax.dot_general(
        left, right, (((1,), (1,)), ((), ())), preferred_element_type=jnp.float32
    )


def dot_nn(left, right):
    return jnp.dot(left, right, preferred_element_type=jnp.float32)


def fourier_table(rows):
    ids = np.arange(rows)
    phase = 2.0 * np.pi * (np.outer(ids, ids) % rows) / rows
    return np.stack(split_const(np.cos(phase)) + split_const(np.sin(phase)))


def sinc_value(offset):
    return math.sin(math.pi * offset) / (math.pi * offset)


def tap_weight(offset):
    return sinc_value(offset - 0.5) * sinc_value((offset - 0.5) / TAPS)


def refine_table(length):
    table = np.zeros((length, 2 * length))
    for m in range(length):
        table[m, 2 * m] = 1.0
        for offset in range(1 - TAPS, TAPS + 1):
            if 0 <= m + offset < length:
                table[m + offset, 2 * m + 1] = tap_weight(offset)
    return np.stack(split_const(table))


def edge_table(length, slabs):
    side = np.zeros((2, TILE, LANES))
    for h in range(TAPS):
        for column in range(LANES):
            if column % 2 == 0:
                continue
            m = (2 * length - LANES + column) // 2
            offset = length + h - m
            if 1 - TAPS <= offset <= TAPS:
                side[0, h, column] = tap_weight(offset)
            m = column // 2
            offset = h - TAPS - m
            if 1 - TAPS <= offset <= TAPS:
                side[1, h, column] = tap_weight(offset)
    full = np.zeros((2, slabs * TILE, slabs * LANES))
    for slab in range(slabs):
        full[:, slab * TILE : (slab + 1) * TILE, slab * LANES : (slab + 1) * LANES] = side
    high, low = split_const(full)
    return np.stack([high, low], axis=1)


class Shape:
    def __init__(self, rows, slabs, length):
        self.rows = rows
        self.slabs = slabs
        self.length = length
        self.block = rows // slabs
        self.tiles = length // TILE + 1
        self.halves = length // LANES


def prepare(shape, order_ref, turn_re, turn_im, wave_re, wave_im, base_t):
    rows = shape.rows
    modulus = float(shape.slabs * rows + 1)
    order_row = order_ref[...].astype(jnp.float32)
    term = lax.broadcasted_iota(jnp.int32, (MAXN, rows), 0).astype(jnp.float32)
    base = term * modulus + order_row
    log_turn = jnp.log(base) * (1.0 / (2.0 * math.pi))
    amp = lax.rsqrt(base)
    step_sin, step_cos = sincos_turns(log_turn * (TILE / 16.0))
    offsets = lax.broadcasted_iota(jnp.int32, (TILE, rows), 0).astype(jnp.float32)
    t_first = (base_t + offsets) * 0.0625
    for n in range(MAXN):
        sin, cos = sincos_turns(t_first * log_turn[n : n + 1, :])
        amp_row = amp[n : n + 1, :]
        wave_re[n] = amp_row * cos
        wave_im[n] = -amp_row * sin
        turn_re[n] = jnp.broadcast_to(step_cos[n : n + 1, :], (TILE, rows))
        turn_im[n] = jnp.broadcast_to(-step_sin[n : n + 1, :], (TILE, rows))


def sum_tiles(shape, first, count, order_ref, counts, turn_re, turn_im, wave_re, wave_im, zeta_re, zeta_im, base_t):
    modulus = float(shape.slabs * shape.rows + 1)
    row0 = first * TILE

    def lane_block(block, carry):
        lanes = pl.ds(pl.multiple_of(block * LANES, LANES), LANES)
        limits = [counts[row0 + a * TILE : row0 + (a + 1) * TILE, :] for a in range(count)]

        def term(n, sums):
            now_re = wave_re[n, :, lanes]
            now_im = wave_im[n, :, lanes]
            rot_re = turn_re[n, :, lanes]
            rot_im = turn_im[n, :, lanes]
            n_float = lax.convert_element_type(n, jnp.float32)
            out = []
            for a in range(count):
                active = limits[a] > n_float
                out.append(sums[2 * a] + jnp.where(active, now_re, 0.0))
                out.append(sums[2 * a + 1] + jnp.where(active, now_im, 0.0))
                now_re, now_im = (
                    now_re * rot_re - now_im * rot_im,
                    now_re * rot_im + now_im * rot_re,
                )
            wave_re[n, :, lanes] = now_re
            wave_im[n, :, lanes] = now_im
            return tuple(out)

        zero = jnp.zeros((TILE, LANES), jnp.float32)
        sums = lax.fori_loop(0, MAXN, term, (zero,) * (2 * count), unroll=4)
        residue = jnp.broadcast_to(order_ref[:, lanes].astype(jnp.float32), (TILE, LANES))
        fraction = residue * (1.0 / modulus)
        offsets = lax.broadcasted_iota(jnp.int32, (TILE, LANES), 0).astype(jnp.float32)
        for a in range(count):
            limit = limits[a]
            t_now = (base_t + float(row0 + a * TILE) + offsets) * 0.0625
            t_square = t_now * t_now
            inverse_den = 1.0 / (0.25 + t_square)
            cubic_re = 1.875 - 4.5 * t_square
            cubic_im = t_now * (5.75 - t_square)
            whole_base = limit * modulus + residue
            tail_base = limit + fraction
            inverse = 1.0 / tail_base
            cube = inverse * inverse * inverse * (1.0 / 720.0)
            twelfth = inverse * (1.0 / 12.0)
            lifted = tail_base * inverse_den
            gain_re = 0.5 + 0.5 * twelfth - 0.5 * lifted - cubic_re * cube
            gain_im = t_now * (twelfth - lifted) - cubic_im * cube
            sin, cos = sincos_turns(t_now * (jnp.log(whole_base) * (1.0 / (2.0 * math.pi))))
            amp = lax.rsqrt(whole_base)
            power_re = amp * cos
            power_im = -amp * sin
            place = slice(row0 + a * TILE, row0 + (a + 1) * TILE)
            zeta_re[place, lanes] = sums[2 * a] + (gain_re * power_re - gain_im * power_im)
            zeta_im[place, lanes] = sums[2 * a + 1] + (gain_re * power_im + gain_im * power_re)
        return carry

    lax.fori_loop(0, shape.rows // LANES, lane_block, 0)


def make_twist(shape, slab_index, twist_cos, twist_sin):
    ids = lax.broadcasted_iota(jnp.int32, (shape.rows, LANES), 0)
    turns = (ids * slab_index).astype(jnp.float32) * (1.0 / (shape.slabs * shape.rows))
    sin, cos = sincos_turns(turns)
    twist_cos[...] = cos
    twist_sin[...] = sin


def transform_half(shape, half, skip, zeta_re, zeta_im, tables, twist_cos, twist_sin, store):
    place = pl.ds(pl.multiple_of(half * LANES + skip, TILE), LANES)
    both = jnp.concatenate([zeta_re[place, :], zeta_im[place, :]], axis=0)
    high, low = split_bf16(both)
    chunk = 2 * shape.block
    for piece in range(shape.rows // chunk):
        rows = slice(piece * chunk, (piece + 1) * chunk)
        cos_high = tables[0, rows, :]
        sin_high = tables[2, rows, :]
        with_cos = dot_nt(cos_high, high) + dot_nt(cos_high, low) + dot_nt(tables[1, rows, :], high)
        with_sin = dot_nt(sin_high, high) + dot_nt(sin_high, low) + dot_nt(tables[3, rows, :], high)
        mixed_re = with_cos[:, :LANES] - with_sin[:, LANES:]
        mixed_im = with_sin[:, :LANES] + with_cos[:, LANES:]
        t_cos = twist_cos[rows, :]
        t_sin = twist_sin[rows, :]
        out_re = t_cos * mixed_re - t_sin * mixed_im
        out_im = t_sin * mixed_re + t_cos * mixed_im
        for sub in range(2):
            cut = slice(sub * shape.block, (sub + 1) * shape.block)
            store(2 * piece + sub, 0, out_re[cut])
            store(2 * piece + sub, 1, out_im[cut])


def transform_edge(shape, place, slab_index, zeta_re, zeta_im, tables, store):
    both = jnp.concatenate([zeta_re[place, :], zeta_im[place, :]], axis=0)
    high, low = split_bf16(both)
    with_cos = dot_nn(high, tables[0]) + dot_nn(low, tables[0]) + dot_nn(high, tables[1])
    with_sin = dot_nn(high, tables[2]) + dot_nn(low, tables[2]) + dot_nn(high, tables[3])
    mixed_re = with_cos[:TILE] - with_sin[TILE:]
    mixed_im = with_sin[:TILE] + with_cos[TILE:]
    ids = lax.broadcasted_iota(jnp.int32, (TILE, shape.rows), 1)
    sin, cos = sincos_turns(
        (ids * slab_index).astype(jnp.float32) * (1.0 / (shape.slabs * shape.rows))
    )
    out_re = cos * mixed_re - sin * mixed_im
    out_im = sin * mixed_re + cos * mixed_im
    lane = lax.broadcasted_iota(jnp.int32, (TILE, LANES), 1)
    for pair in range(shape.slabs // 2):
        cut = slice(pair * LANES, (pair + 1) * LANES)
        part_re = out_re[:, cut]
        part_im = out_im[:, cut]
        store(2 * pair, jnp.where(lane < LANES // 2, part_re, pltpu.roll(part_im, LANES // 2, 1)))
        store(
            2 * pair + 1,
            jnp.where(lane < LANES // 2, pltpu.roll(part_re, LANES // 2, 1), part_im),
        )


def column_counts(shape, own_row, other_row, own_at, other_from, other_at, counts, spare):
    def columns(row_ref, cut):
        lanes = slice(cut * LANES, (cut + 1) * LANES)
        return jnp.broadcast_to(row_ref[:, lanes].astype(jnp.float32), (LANES, LANES)).T

    for cut in range(shape.halves):
        at = pl.ds(pl.multiple_of(own_at + cut * LANES, TILE), LANES)
        counts[at, :] = columns(own_row, cut)
        spare[cut * LANES : (cut + 1) * LANES, :] = columns(other_row, cut)
    counts[pl.ds(pl.multiple_of(other_at, TILE), TILE), :] = spare[
        pl.ds(pl.multiple_of(other_from, TILE), TILE), :
    ]


def zeta_kernel(shape, start_ref, order_ref, count_ref, table_hbm, main_out, edge_out, main_send, edge_send,
                other_counts, spare, tables, turn_re, turn_im, wave_re, wave_im, zeta_re, zeta_im, counts,
                twist_cos, twist_sin, table_sem, count_sems, main_send_sems, main_recv_sems,
                edge_send_sems, edge_recv_sems):
    slabs, length = shape.slabs, shape.length
    me = lax.axis_index("res")
    ta_index = lax.axis_index("ta")
    mesh_ids = pl.DeviceIdType.MESH
    peers = [lax.rem(me + d, slabs) for d in range(slabs)]

    barrier = pltpu.get_barrier_semaphore()
    for d in range(1, slabs):
        pl.semaphore_signal(barrier, inc=1, device_id={"res": peers[d]}, device_id_type=mesh_ids)
    pl.semaphore_signal(barrier, inc=1, device_id={"ta": 1 - ta_index}, device_id_type=mesh_ids)
    table_copy = pltpu.make_async_copy(table_hbm, tables, table_sem)
    table_copy.start()

    base_t = (start_ref[0] + ta_index * (length - TILE)).astype(jnp.float32)
    make_twist(shape, me, twist_cos, twist_sin)
    pl.semaphore_wait(barrier, slabs)
    count_copy = pltpu.make_async_remote_copy(
        src_ref=count_ref, dst_ref=other_counts, send_sem=count_sems.at[0], recv_sem=count_sems.at[1],
        device_id={"ta": 1 - ta_index}, device_id_type=mesh_ids,
    )
    count_copy.start()
    prepare(shape, order_ref, turn_re, turn_im, wave_re, wave_im, base_t)
    count_copy.wait()
    column_counts(shape, count_ref, other_counts, ta_index * TILE, ta_index * (length - TILE),
                  (1 - ta_index) * length, counts, spare)

    copies = []

    def send(source, target, send_sems, recv_sems, d):
        copy = pltpu.make_async_remote_copy(
            src_ref=source, dst_ref=target, send_sem=send_sems, recv_sem=recv_sems,
            device_id={"res": peers[d]}, device_id_type=mesh_ids,
        )
        copy.start()
        copies.append(copy)

    first = 0
    for half in range(shape.halves):
        for count in ((9, 8) if half == 0 else (8, 8)):
            sum_tiles(shape, first, count, order_ref, counts, turn_re, turn_im, wave_re, wave_im,
                      zeta_re, zeta_im, base_t)
            first += count
        if half == 0:
            table_copy.wait()

        def store(block, part, values, half=half):
            main_send[half, block, part] = values

        transform_half(shape, half, ta_index * TILE, zeta_re, zeta_im, tables, twist_cos, twist_sin, store)
        for d in range(1, slabs):
            send(main_send.at[half, peers[d]], main_out.at[half, me],
                 main_send_sems.at[half, d], main_recv_sems.at[half, d], d)
        main_out[half, me] = main_send[half, me]

    def store_edge(block, values):
        edge_send[block] = values

    edge_place = pl.ds(pl.multiple_of((1 - ta_index) * length, TILE), TILE)
    transform_edge(shape, edge_place, me, zeta_re, zeta_im, tables, store_edge)
    for d in range(1, slabs):
        send(edge_send.at[peers[d]], edge_out.at[me], edge_send_sems.at[d], edge_recv_sems.at[d], d)
    edge_out[me] = edge_send[me]
    for copy in copies:
        copy.wait()


def turn_eighth(re, im, eighths):
    root = math.sqrt(0.5)
    if eighths == 0:
        return re, im
    if eighths == 1:
        return root * (re - im), root * (re + im)
    if eighths == 2:
        return -im, re
    return -root * (re + im), root * (re - im)


def fft_eight(parts):
    def step(values):
        size = len(values)
        if size == 1:
            return values
        even = step(values[0::2])
        odd = step(values[1::2])
        low, high = [], []
        for k in range(size // 2):
            o_re, o_im = turn_eighth(*odd[k], k * (8 // size))
            e_re, e_im = even[k]
            low.append((e_re + o_re, e_im + o_im))
            high.append((e_re - o_re, e_im - o_im))
        return low + high

    return step(parts)


def refine_kernel(shape, chunk, main_ref, edge_ref, table, edge_tab, out_ref, edge_out):
    step = pl.program_id(0)
    slabs = shape.slabs
    half_lanes = LANES // 2
    ta_index = lax.axis_index("ta")

    @pl.when(step == 0)
    def _():
        lane = lax.broadcasted_iota(jnp.int32, (TILE, LANES), 1)
        parts = [(edge_ref[p], pltpu.roll(edge_ref[p], half_lanes, 1)) for p in range(slabs)]
        mixed = fft_eight(parts)
        rows = [jnp.where(lane < half_lanes, re, pltpu.roll(im, half_lanes, 1)) for re, im in mixed]
        stacked = jnp.concatenate(rows + rows, axis=0)
        high, low = split_bf16(stacked.T[:, : slabs * TILE])
        tab_high = edge_tab[ta_index, 0]
        tab_low = edge_tab[ta_index, 1]
        edge_out[...] = dot_nn(high, tab_high) + dot_nn(low, tab_high) + dot_nn(high, tab_low)

    parts = []
    for p in range(slabs):
        re = jnp.concatenate([main_ref[h, p, 0] for h in range(shape.halves)], axis=1)
        im = jnp.concatenate([main_ref[h, p, 1] for h in range(shape.halves)], axis=1)
        parts.append((re, im))
    mixed = fft_eight(parts)
    stacked = jnp.concatenate([m[0] for m in mixed] + [m[1] for m in mixed], axis=0)
    high, low = split_bf16(stacked)
    result = dot_nn(high, table[0]) + dot_nn(low, table[0]) + dot_nn(high, table[1])
    edge_lanes = pl.ds(
        pl.multiple_of((1 - ta_index) * (2 * shape.length - LANES), LANES), LANES
    )
    for part in range(2):
        rows = pl.ds(pl.multiple_of(part * shape.block + step * chunk, TILE), chunk)
        for w in range(slabs):
            at = (part * slabs + w) * chunk
            out_ref[part, w] = result[at : at + chunk]
            out_ref[part, w, :, edge_lanes] += edge_out[rows, w * LANES : (w + 1) * LANES]


def fast_device(log_order, t_start, term_counts):
    shape = Shape(log_order.shape[1], lax.axis_size("res"), term_counts.shape[0])
    rows, slabs, length = shape.rows, shape.slabs, shape.length
    f32 = jnp.float32
    vmem = pl.BlockSpec(memory_space=pltpu.VMEM)
    main_shape = (shape.halves, slabs, 2, shape.block, LANES)
    edge_shape = (slabs, TILE, LANES)
    table = fourier_table(rows)
    main, edge = pl.pallas_call(
        functools.partial(zeta_kernel, shape),
        out_shape=(jax.ShapeDtypeStruct(main_shape, f32), jax.ShapeDtypeStruct(edge_shape, f32)),
        in_specs=[pl.BlockSpec(memory_space=pltpu.SMEM), vmem, vmem, pl.BlockSpec(memory_space=pltpu.HBM)],
        out_specs=(vmem, vmem),
        scratch_shapes=[
            pltpu.VMEM(main_shape, f32),
            pltpu.VMEM(edge_shape, f32),
            pltpu.VMEM((1, length), jnp.int32),
            pltpu.VMEM((length, LANES), f32),
            pltpu.VMEM(table.shape, jnp.bfloat16),
            pltpu.VMEM((MAXN, TILE, rows), f32),
            pltpu.VMEM((MAXN, TILE, rows), f32),
            pltpu.VMEM((MAXN, TILE, rows), f32),
            pltpu.VMEM((MAXN, TILE, rows), f32),
            pltpu.VMEM((length + TILE, rows), f32),
            pltpu.VMEM((length + TILE, rows), f32),
            pltpu.VMEM((length + TILE, LANES), f32),
            pltpu.VMEM((rows, LANES), f32),
            pltpu.VMEM((rows, LANES), f32),
            pltpu.SemaphoreType.DMA,
            pltpu.SemaphoreType.DMA((2,)),
            pltpu.SemaphoreType.DMA((shape.halves, slabs)),
            pltpu.SemaphoreType.DMA((shape.halves, slabs)),
            pltpu.SemaphoreType.DMA((slabs,)),
            pltpu.SemaphoreType.DMA((slabs,)),
        ],
        compiler_params=pltpu.CompilerParams(
            collective_id=0, has_side_effects=True, vmem_limit_bytes=48 * 2**20
        ),
    )(t_start, log_order, term_counts[None, :], jnp.asarray(table))
    return refine_call(shape, main, edge)


def refine_call(shape, main, edge):
    slabs, length = shape.slabs, shape.length
    chunk = 16
    f32 = jnp.float32
    return pl.pallas_call(
        functools.partial(refine_kernel, shape, chunk),
        grid=(shape.block // chunk,),
        out_shape=jax.ShapeDtypeStruct((2, slabs, shape.block, 2 * length), f32),
        in_specs=[
            pl.BlockSpec((shape.halves, slabs, 2, chunk, LANES), lambda i: (0, 0, 0, i, 0)),
            pl.BlockSpec((slabs, TILE, LANES), lambda i: (0, 0, 0)),
            pl.BlockSpec((2, length, 2 * length), lambda i: (0, 0, 0)),
            pl.BlockSpec((2, 2, slabs * TILE, slabs * LANES), lambda i: (0, 0, 0, 0)),
        ],
        out_specs=pl.BlockSpec((2, slabs, chunk, 2 * length), lambda i: (0, 0, i, 0)),
        scratch_shapes=[pltpu.VMEM((LANES, slabs * LANES), f32)],
        compiler_params=pltpu.CompilerParams(vmem_limit_bytes=48 * 2**20),
    )(main, edge, jnp.asarray(refine_table(length)), jnp.asarray(edge_table(length, slabs)))


time_step = 0.0625


def padded_2(block, sides, width):
    for axis, dim in sides:
        count = lax.axis_size(axis)
        forward = [(i, i + 1) for i in range(count - 1)]
        backward = [(target, source) for source, target in forward]
        low = lax.ppermute(
            lax.slice_in_dim(block, block.shape[dim] - width, None, axis=dim), axis, forward
        )
        high = lax.ppermute(lax.slice_in_dim(block, 0, width, axis=dim), axis, backward)
        block = jnp.concatenate([low, block, high], axis=dim)
    return block


def inverse_power(base_value, t_values):
    modulus = lax.rsqrt(base_value)
    phase_now = t_values * jnp.log(base_value)
    return (modulus * jnp.cos(phase_now), -modulus * jnp.sin(phase_now))


def hurwitz_values(x_values, t_values, count_row, most_terms):
    shape_out = (x_values.shape[0], t_values.shape[1])

    def add_term(term_index, running):
        sum_re, sum_im = running
        base_value = term_index.astype(x_values.dtype) + x_values
        piece_re, piece_im = inverse_power(base_value, t_values)
        active = term_index < count_row
        return (
            sum_re + jnp.where(active, piece_re, 0.0),
            sum_im + jnp.where(active, piece_im, 0.0),
        )

    zeros_init = jnp.zeros(shape_out, x_values.dtype)
    sum_re, sum_im = lax.fori_loop(0, most_terms, add_term, (zeros_init, zeros_init))
    tail_base = count_row.astype(x_values.dtype) + x_values
    power_re, power_im = inverse_power(tail_base, t_values)
    denominator = 0.25 + t_values * t_values
    lifted_re = tail_base * power_re
    lifted_im = tail_base * power_im
    total_re = sum_re + (-0.5 * lifted_re + t_values * lifted_im) / denominator + 0.5 * power_re
    total_im = sum_im + (-t_values * lifted_re - 0.5 * lifted_im) / denominator + 0.5 * power_im
    total_re = total_re + (0.5 * power_re - t_values * power_im) / (12.0 * tail_base)
    total_im = total_im + (0.5 * power_im + t_values * power_re) / (12.0 * tail_base)
    cubic_re = 1.875 - 4.5 * t_values * t_values
    cubic_im = 5.75 * t_values - t_values * t_values * t_values
    cube_base = 720.0 * tail_base * tail_base * tail_base
    total_re = total_re - (cubic_re * power_re - cubic_im * power_im) / cube_base
    total_im = total_im - (cubic_re * power_im + cubic_im * power_re) / cube_base
    return (total_re, total_im)


def refine(padded, half_width, length):
    coarse = padded[..., half_width : half_width + length]
    middle = jnp.zeros_like(coarse)
    for offset in range(1 - half_width, half_width + 1):
        weight = sinc_value(offset - 0.5) * sinc_value((offset - 0.5) / half_width)
        middle = middle + weight * padded[..., half_width + offset : half_width + offset + length]
    stacked = jnp.stack([coarse, middle], axis=-1)
    return stacked.reshape(stacked.shape[:-2] + (2 * length,))


def matmul_high(left, right):
    return jnp.dot(left, right, precision=lax.Precision.HIGHEST, preferred_element_type=jnp.float32)


def per_device(log_order, t_start, term_counts):
    rows_here = log_order.shape[1]
    slabs = lax.axis_size("res")
    slab_index = lax.axis_index("res")
    length_here = term_counts.shape[0]
    ta_index = lax.axis_index("ta")
    modulus_int = slabs * rows_here + 1
    x_values = log_order.reshape(rows_here, 1).astype(jnp.float32) / jnp.float32(modulus_int)
    row_ids = jnp.arange(rows_here, dtype=jnp.int32)
    first_phase = (row_ids[:, None] * row_ids[None, :] % rows_here).astype(jnp.float32) * (
        2.0 * math.pi / rows_here
    )
    first_cos = jnp.cos(first_phase)
    first_sin = jnp.sin(first_phase)
    twist_phase = (row_ids * slab_index).astype(jnp.float32)[:, None] * (
        2.0 * math.pi / (slabs * rows_here)
    )
    twist_cos = jnp.cos(twist_phase)
    twist_sin = jnp.sin(twist_phase)
    slab_ids = jnp.arange(slabs, dtype=jnp.int32)
    second_phase = (slab_ids[:, None] * slab_ids[None, :] % slabs).astype(jnp.float32) * (
        2.0 * math.pi / slabs
    )
    second_cos = jnp.cos(second_phase)
    second_sin = jnp.sin(second_phase)
    positions = ta_index * length_here + jnp.arange(length_here, dtype=jnp.int32)
    count_row = term_counts[None, :]
    t_values = ((t_start[0] + positions).astype(jnp.float32) * time_step)[None, :]
    zeta_re, zeta_im = hurwitz_values(x_values, t_values, count_row, MAXN)
    mixed_re = matmul_high(first_cos, zeta_re) - matmul_high(first_sin, zeta_im)
    mixed_im = matmul_high(first_sin, zeta_re) + matmul_high(first_cos, zeta_im)
    turned_re = twist_cos * mixed_re - twist_sin * mixed_im
    turned_im = twist_sin * mixed_re + twist_cos * mixed_im
    sectioned = jnp.stack([turned_re, turned_im])[:, None]
    block_in = lax.all_to_all(sectioned, "res", split_axis=2, concat_axis=1, tiled=True)
    part_re = block_in[0]
    part_im = block_in[1]

    def mix(table, values):
        return jnp.einsum(
            "wp,psn->wsn",
            table,
            values,
            precision=lax.Precision.HIGHEST,
            preferred_element_type=jnp.float32,
        )

    out_re = mix(second_cos, part_re) - mix(second_sin, part_im)
    out_im = mix(second_sin, part_re) + mix(second_cos, part_im)
    spectrum = jnp.stack([out_re, out_im])
    factor_re, factor_im = inverse_power(jnp.float32(modulus_int), t_values)
    lval_re = spectrum[0] * factor_re - spectrum[1] * factor_im
    lval_im = spectrum[0] * factor_im + spectrum[1] * factor_re
    lvals = jnp.stack([lval_re, lval_im])
    padded = padded_2(lvals, (("ta", 3),), TAPS)
    return refine(padded, TAPS, length_here)


def solution(mesh):
    placed = (P("res", None), P("grp"), P(("grp", "ta")))
    return jax.shard_map(
        fast_device if mesh.shape["res"] == 8 and mesh.shape["ta"] == 2 else per_device,
        mesh=mesh,
        in_specs=placed,
        out_specs=P(None, None, "res", ("grp", "ta")),
        check_vma=False,
    )
```

```python
import functools
import math

import jax
import jax.numpy as jnp
import ml_dtypes
import numpy as np
from jax import lax
from jax.experimental import pallas as pl
from jax.experimental.pallas import tpu as pltpu
from jax.sharding import PartitionSpec as P

TAPS = 8
MAXN = 32
NMIN = 4
LANES = 128
HALF = LANES // 2
PEER_ORDER = (6, 7, 4, 5, 2, 3, 1)
NEAR_ORDER = (2, 3, 1)
TWICE = 2
TILE = 8

SIN_COEFS = (
    6.2831854820251465, -41.34170150756836, 81.60513305664062, -76.7030029296875,
    42.02585220336914, -14.899578094482422, 3.2377800941467285,
)
COS_COEFS = (
    1.0, -19.73920440673828, 64.93911743164062, -85.45011138916016,
    60.16743087768555, -25.96688461303711, 6.527706146240234,
)
ROUNDER = 12582912.0


def sincos_turns(turns):
    frac = turns - ((turns + ROUNDER) - ROUNDER)
    square = frac * frac
    sin_acc = jnp.full_like(square, SIN_COEFS[-1])
    cos_acc = jnp.full_like(square, COS_COEFS[-1])
    for sin_c, cos_c in zip(SIN_COEFS[-2::-1], COS_COEFS[-2::-1]):
        sin_acc = sin_acc * square + sin_c
        cos_acc = cos_acc * square + cos_c
    return sin_acc * frac, cos_acc


def split_bf16(values):
    high = values.astype(jnp.bfloat16)
    return high, (values - high.astype(jnp.float32)).astype(jnp.bfloat16)


def split_const(values):
    high = values.astype(np.float32).astype(ml_dtypes.bfloat16)
    low = (values - high.astype(np.float64)).astype(np.float32).astype(ml_dtypes.bfloat16)
    return high, low


def dot_nt(left, right):
    return lax.dot_general(
        left, right, (((1,), (1,)), ((), ())), preferred_element_type=jnp.float32
    )


def dot_nn(left, right):
    return jnp.dot(left, right, preferred_element_type=jnp.float32)


def fourier_table(rows):
    ids = np.arange(rows)
    phase = 2.0 * np.pi * (np.outer(ids, ids) % rows) / rows
    return np.stack(split_const(np.cos(phase)) + split_const(np.sin(phase)))


def sinc_value(offset):
    return math.sin(math.pi * offset) / (math.pi * offset)


def tap_weight(offset):
    return sinc_value(offset - 0.5) * sinc_value((offset - 0.5) / TAPS)


def refine_table(length):
    table = np.zeros((length, 2 * length))
    for m in range(length):
        table[m, 2 * m] = 1.0
        for offset in range(1 - TAPS, TAPS + 1):
            if 0 <= m + offset < length:
                table[m + offset, 2 * m + 1] = tap_weight(offset)
    return np.stack(split_const(table))


def edge_table(length, slabs):
    side = np.zeros((2, TILE, LANES))
    for h in range(TAPS):
        for column in range(LANES):
            if column % 2 == 0:
                continue
            m = (2 * length - LANES + column) // 2
            offset = length + h - m
            if 1 - TAPS <= offset <= TAPS:
                side[0, h, column] = tap_weight(offset)
            m = column // 2
            offset = h - TAPS - m
            if 1 - TAPS <= offset <= TAPS:
                side[1, h, column] = tap_weight(offset)
    full = np.zeros((2, slabs * TILE, slabs * LANES))
    for slab in range(slabs):
        full[:, slab * TILE : (slab + 1) * TILE, slab * LANES : (slab + 1) * LANES] = side
    high, low = split_const(full)
    return np.stack([high, low], axis=1)


class Shape:
    def __init__(self, rows, slabs, length):
        self.rows = rows
        self.slabs = slabs
        self.length = length
        self.block = rows // slabs
        self.tiles = length // TILE + 1
        self.halves = length // LANES
        self.chunks = length // HALF


def prepare(shape, order_ref, turn_re, turn_im, wave_re, wave_im, base_t):
    rows = shape.rows
    modulus = float(shape.slabs * rows + 1)
    order_row = order_ref[...].astype(jnp.float32)
    term = lax.broadcasted_iota(jnp.int32, (MAXN, rows), 0).astype(jnp.float32)
    base = term * modulus + order_row
    log_turn = jnp.log(base) * (1.0 / (2.0 * math.pi))
    amp = lax.rsqrt(base)
    step_sin, step_cos = sincos_turns(log_turn * (TILE / 16.0))
    offsets = lax.broadcasted_iota(jnp.int32, (TILE, rows), 0).astype(jnp.float32)
    t_first = (base_t + offsets) * 0.0625
    for n in range(MAXN):
        sin, cos = sincos_turns(t_first * log_turn[n : n + 1, :])
        amp_row = amp[n : n + 1, :]
        wave_re[n] = amp_row * cos
        wave_im[n] = -amp_row * sin
        turn_re[n] = jnp.broadcast_to(step_cos[n : n + 1, :], (TILE, rows))
        turn_im[n] = jnp.broadcast_to(-step_sin[n : n + 1, :], (TILE, rows))


def sum_tiles(shape, first, count, order_ref, counts, turn_re, turn_im, wave_re, wave_im, zeta_re, zeta_im, base_t):
    modulus = float(shape.slabs * shape.rows + 1)
    row0 = first * TILE

    def lane_block(block, carry):
        lanes = pl.ds(pl.multiple_of(block * LANES, LANES), LANES)
        limits = [counts[row0 + a * TILE : row0 + (a + 1) * TILE, :] for a in range(count)]

        def term(n, sums, masked):
            now_re = wave_re[n, :, lanes]
            now_im = wave_im[n, :, lanes]
            rot_re = turn_re[n, :, lanes]
            rot_im = turn_im[n, :, lanes]
            twice_cos = rot_re + rot_re
            last_re = last_im = None
            out = []
            for a in range(count):
                if masked:
                    active = limits[a] > lax.convert_element_type(n, jnp.float32)
                    out.append(sums[2 * a] + jnp.where(active, now_re, 0.0))
                    out.append(sums[2 * a + 1] + jnp.where(active, now_im, 0.0))
                else:
                    out.append(sums[2 * a] + now_re)
                    out.append(sums[2 * a + 1] + now_im)
                if a == 0:
                    next_re = now_re * rot_re - now_im * rot_im
                    next_im = now_re * rot_im + now_im * rot_re
                else:
                    next_re = twice_cos * now_re - last_re
                    next_im = twice_cos * now_im - last_im
                last_re, last_im, now_re, now_im = now_re, now_im, next_re, next_im
            wave_re[n, :, lanes] = now_re
            wave_im[n, :, lanes] = now_im
            return tuple(out)

        sums = (jnp.zeros((TILE, LANES), jnp.float32),) * (2 * count)
        for n in range(NMIN):
            sums = term(n, sums, False)
        sums = lax.fori_loop(NMIN, MAXN, functools.partial(term, masked=True), sums, unroll=4)
        residue = jnp.broadcast_to(order_ref[:, lanes].astype(jnp.float32), (TILE, LANES))
        fraction = residue * (1.0 / modulus)
        offsets = lax.broadcasted_iota(jnp.int32, (TILE, LANES), 0).astype(jnp.float32)
        for a in range(count):
            limit = limits[a]
            t_now = (base_t + float(row0 + a * TILE) + offsets) * 0.0625
            t_square = t_now * t_now
            inverse_den = 1.0 / (0.25 + t_square)
            cubic_re = 1.875 - 4.5 * t_square
            cubic_im = t_now * (5.75 - t_square)
            whole_base = limit * modulus + residue
            tail_base = limit + fraction
            inverse = 1.0 / tail_base
            cube = inverse * inverse * inverse * (1.0 / 720.0)
            twelfth = inverse * (1.0 / 12.0)
            lifted = tail_base * inverse_den
            gain_re = 0.5 + 0.5 * twelfth - 0.5 * lifted - cubic_re * cube
            gain_im = t_now * (twelfth - lifted) - cubic_im * cube
            sin, cos = sincos_turns(t_now * (jnp.log(whole_base) * (1.0 / (2.0 * math.pi))))
            amp = lax.rsqrt(whole_base)
            power_re = amp * cos
            power_im = -amp * sin
            place = slice(row0 + a * TILE, row0 + (a + 1) * TILE)
            zeta_re[place, lanes] = sums[2 * a] + (gain_re * power_re - gain_im * power_im)
            zeta_im[place, lanes] = sums[2 * a + 1] + (gain_re * power_im + gain_im * power_re)
        return carry

    lax.fori_loop(0, shape.rows // LANES, lane_block, 0)


def make_twist(shape, slab_index, twist_cos, twist_sin):
    ids = lax.broadcasted_iota(jnp.int32, (shape.rows, LANES), 0)
    turns = (ids * slab_index).astype(jnp.float32) * (1.0 / (shape.slabs * shape.rows))
    sin, cos = sincos_turns(turns)
    twist_cos[...] = cos
    twist_sin[...] = sin


def transform_chunk(shape, chunk, skip, first_block, blocks, zeta_re, zeta_im, tables, twist_cos, twist_sin, store):
    place = pl.ds(pl.multiple_of(chunk * HALF + skip, TILE), HALF)
    high, low = split_bf16(jnp.concatenate([zeta_re[place, :], zeta_im[place, :]], axis=0))
    both = jnp.concatenate([high, low], axis=0)
    cut_rows = 2 * shape.block
    lane = lax.broadcasted_iota(jnp.int32, (cut_rows, LANES), 1)
    sign = jnp.where(lane < HALF, -1.0, 1.0)
    for piece in range(blocks // 2):
        start = first_block * shape.block + piece * cut_rows
        rows = pl.ds(pl.multiple_of(start, cut_rows), cut_rows)
        with_cos = dot_nt(tables[0, rows, :], both)
        with_sin = dot_nt(tables[2, rows, :], both)
        with_cos = with_cos[:, :LANES] + with_cos[:, LANES:] + dot_nt(tables[1, rows, :], high)
        with_sin = with_sin[:, :LANES] + with_sin[:, LANES:] + dot_nt(tables[3, rows, :], high)
        mixed = with_cos + sign * pltpu.roll(with_sin, HALF, 1)
        out = twist_cos[rows, :] * mixed + (sign * twist_sin[rows, :]) * pltpu.roll(mixed, HALF, 1)
        for sub in range(2):
            store(2 * piece + sub, out[sub * shape.block : (sub + 1) * shape.block])


def transform_edge(shape, place, slab_index, zeta_re, zeta_im, tables, store):
    both = jnp.concatenate([zeta_re[place, :], zeta_im[place, :]], axis=0)
    high, low = split_bf16(both)
    with_cos = dot_nn(high, tables[0]) + dot_nn(low, tables[0]) + dot_nn(high, tables[1])
    with_sin = dot_nn(high, tables[2]) + dot_nn(low, tables[2]) + dot_nn(high, tables[3])
    mixed_re = with_cos[:TILE] - with_sin[TILE:]
    mixed_im = with_sin[:TILE] + with_cos[TILE:]
    ids = lax.broadcasted_iota(jnp.int32, (TILE, shape.rows), 1)
    sin, cos = sincos_turns(
        (ids * slab_index).astype(jnp.float32) * (1.0 / (shape.slabs * shape.rows))
    )
    out_re = cos * mixed_re - sin * mixed_im
    out_im = sin * mixed_re + cos * mixed_im
    lane = lax.broadcasted_iota(jnp.int32, (TILE, LANES), 1)
    for pair in range(shape.slabs // 2):
        cut = slice(pair * LANES, (pair + 1) * LANES)
        part_re = out_re[:, cut]
        part_im = out_im[:, cut]
        store(2 * pair, jnp.where(lane < LANES // 2, part_re, pltpu.roll(part_im, LANES // 2, 1)))
        store(
            2 * pair + 1,
            jnp.where(lane < LANES // 2, pltpu.roll(part_re, LANES // 2, 1), part_im),
        )


def column_counts(shape, own_row, other_row, own_at, other_from, other_at, counts, spare):
    def columns(row_ref, cut):
        lanes = slice(cut * LANES, (cut + 1) * LANES)
        return jnp.broadcast_to(row_ref[:, lanes].astype(jnp.float32), (LANES, LANES)).T

    for cut in range(shape.halves):
        at = pl.ds(pl.multiple_of(own_at + cut * LANES, TILE), LANES)
        counts[at, :] = columns(own_row, cut)
        spare[cut * LANES : (cut + 1) * LANES, :] = columns(other_row, cut)
    counts[pl.ds(pl.multiple_of(other_at, TILE), TILE), :] = spare[
        pl.ds(pl.multiple_of(other_from, TILE), TILE), :
    ]


def flipped(index, bits):
    for bit in (1, 2, 4):
        if bits & bit:
            index = index + bit * (1 - 2 * ((index // bit) % 2))
    return index


def zeta_kernel(shape, start_ref, order_ref, count_ref, table_hbm, main_out, edge_out, main_send, edge_send,
                other_counts, other_order, spare, tables, turn_re, turn_im, wave_re, wave_im, zeta_re, zeta_im, counts,
                twist_cos, twist_sin, table_sem, count_sems, main_send_sems, main_recv_sems,
                edge_send_sems, edge_recv_sems):
    slabs, length = shape.slabs, shape.length
    me = lax.axis_index("res")
    ta_index = lax.axis_index("ta")
    mesh_ids = pl.DeviceIdType.MESH
    peers = [flipped(me, d) for d in range(slabs)]

    barrier = pltpu.get_barrier_semaphore()
    for d in range(1, slabs):
        pl.semaphore_signal(barrier, inc=1, device_id={"res": peers[d]}, device_id_type=mesh_ids)
    pl.semaphore_signal(barrier, inc=1, device_id={"ta": 1 - ta_index}, device_id_type=mesh_ids)
    table_copy = pltpu.make_async_copy(table_hbm, tables, table_sem)
    table_copy.start()

    base_t = (start_ref[0] + ta_index * (length - TILE)).astype(jnp.float32)
    make_twist(shape, me, twist_cos, twist_sin)
    pl.semaphore_wait(barrier, slabs)
    count_copy = pltpu.make_async_remote_copy(
        src_ref=count_ref, dst_ref=other_counts, send_sem=count_sems.at[0], recv_sem=count_sems.at[1],
        device_id={"ta": 1 - ta_index}, device_id_type=mesh_ids,
    )
    count_copy.start()
    order_copy = pltpu.make_async_remote_copy(
        src_ref=order_ref, dst_ref=other_order, send_sem=count_sems.at[2], recv_sem=count_sems.at[3],
        device_id={"res": peers[slabs // 2]}, device_id_type=mesh_ids,
    )
    order_copy.start()
    prepare(shape, order_ref, turn_re, turn_im, wave_re, wave_im, base_t)
    count_copy.wait()
    order_copy.wait()
    column_counts(shape, count_ref, other_counts, ta_index * TILE, ta_index * (length - TILE),
                  (1 - ta_index) * length, counts, spare)

    copies = []

    def send(source, target, send_sems, recv_sems, d):
        copy = pltpu.make_async_remote_copy(
            src_ref=source, dst_ref=target, send_sem=send_sems, recv_sem=recv_sems,
            device_id={"res": peers[d]}, device_id_type=mesh_ids,
        )
        copy.start()
        copies.append(copy)

    def sums_and_blocks(order, chunk, extra, first, blocks, store):
        start = chunk * (HALF // TILE) + (0 if extra else 1)
        sum_tiles(shape, start, HALF // TILE + extra, order, counts, turn_re, turn_im, wave_re, wave_im,
                  zeta_re, zeta_im, base_t)
        if order is order_ref and chunk == 0:
            table_copy.wait()
        transform_chunk(shape, chunk, ta_index * TILE, first, blocks, zeta_re, zeta_im, tables,
                        twist_cos, twist_sin, store)

    near = slabs // 2
    near_first = (me // near) * near
    far_first = near - near_first
    split = shape.chunks - TWICE
    for chunk in range(shape.chunks):
        wide = chunk < split
        first = 0 if wide else near_first

        def store(block, values, chunk=chunk, first=first):
            main_send[chunk, first + block] = values

        sums_and_blocks(order_ref, chunk, int(chunk == 0), first, slabs if wide else near, store)
        for d in PEER_ORDER if wide else NEAR_ORDER:
            send(main_send.at[chunk, peers[d]], main_out.at[chunk, me],
                 main_send_sems.at[chunk, d], main_recv_sems.at[chunk, d], d)
        main_out[chunk, me] = main_send[chunk, me]

    def store_edge(block, values):
        edge_send[block] = values

    edge_place = pl.ds(pl.multiple_of((1 - ta_index) * length, TILE), TILE)
    transform_edge(shape, edge_place, me, zeta_re, zeta_im, tables, store_edge)
    for d in PEER_ORDER:
        send(edge_send.at[peers[d]], edge_out.at[me], edge_send_sems.at[d], edge_recv_sems.at[d], d)
    edge_out[me] = edge_send[me]

    partner = peers[near]
    prepare(shape, other_order, turn_re, turn_im, wave_re, wave_im, base_t + float(split * HALF))
    make_twist(shape, partner, twist_cos, twist_sin)
    for chunk in range(split, shape.chunks):

        def store(block, values, chunk=chunk):
            main_send[chunk, far_first + block] = values

        sums_and_blocks(other_order, chunk, int(chunk == split), near_first, near, store)
        for d in NEAR_ORDER:
            send(main_send.at[chunk, peers[near + d]], main_out.at[chunk, partner],
                 main_send_sems.at[chunk, near + d], main_recv_sems.at[chunk, near + d], d)
        main_out[chunk, partner] = main_send[chunk, partner]
    for copy in copies:
        copy.wait()


def turn_eighth(re, im, eighths):
    root = math.sqrt(0.5)
    if eighths == 0:
        return re, im
    if eighths == 1:
        return root * (re - im), root * (re + im)
    if eighths == 2:
        return -im, re
    return -root * (re + im), root * (re - im)


def fft_eight(parts):
    def step(values):
        size = len(values)
        if size == 1:
            return values
        even = step(values[0::2])
        odd = step(values[1::2])
        low, high = [], []
        for k in range(size // 2):
            o_re, o_im = turn_eighth(*odd[k], k * (8 // size))
            e_re, e_im = even[k]
            low.append((e_re + o_re, e_im + o_im))
            high.append((e_re - o_re, e_im - o_im))
        return low + high

    return step(parts)


def refine_kernel(shape, chunk, main_ref, edge_ref, table, edge_tab, out_ref, edge_out):
    step = pl.program_id(0)
    slabs = shape.slabs
    half_lanes = LANES // 2
    ta_index = lax.axis_index("ta")

    @pl.when(step == 0)
    def _():
        lane = lax.broadcasted_iota(jnp.int32, (TILE, LANES), 1)
        parts = [(edge_ref[p], pltpu.roll(edge_ref[p], half_lanes, 1)) for p in range(slabs)]
        mixed = fft_eight(parts)
        rows = [jnp.where(lane < half_lanes, re, pltpu.roll(im, half_lanes, 1)) for re, im in mixed]
        stacked = jnp.concatenate(rows + rows, axis=0)
        high, low = split_bf16(stacked.T[:, : slabs * TILE])
        tab_high = edge_tab[ta_index, 0]
        tab_low = edge_tab[ta_index, 1]
        edge_out[...] = dot_nn(high, tab_high) + dot_nn(low, tab_high) + dot_nn(high, tab_low)

    low_half = lax.broadcasted_iota(jnp.int32, (chunk, LANES), 1) < half_lanes
    parts = []
    for p in range(slabs):
        re, im = [], []
        for h in range(shape.halves):
            left = main_ref[2 * h, p]
            right = main_ref[2 * h + 1, p]
            re.append(jnp.where(low_half, left, pltpu.roll(right, half_lanes, 1)))
            im.append(jnp.where(low_half, pltpu.roll(left, half_lanes, 1), right))
        parts.append((jnp.concatenate(re, axis=1), jnp.concatenate(im, axis=1)))
    mixed = fft_eight(parts)
    stacked = jnp.concatenate([m[0] for m in mixed] + [m[1] for m in mixed], axis=0)
    high, low = split_bf16(stacked)
    result = dot_nn(high, table[0]) + dot_nn(low, table[0]) + dot_nn(high, table[1])
    edge_lanes = pl.ds(
        pl.multiple_of((1 - ta_index) * (2 * shape.length - LANES), LANES), LANES
    )
    for part in range(2):
        rows = pl.ds(pl.multiple_of(part * shape.block + step * chunk, TILE), chunk)
        for w in range(slabs):
            at = (part * slabs + w) * chunk
            out_ref[part, w] = result[at : at + chunk]
            out_ref[part, w, :, edge_lanes] += edge_out[rows, w * LANES : (w + 1) * LANES]


def fast_device(log_order, t_start, term_counts):
    shape = Shape(log_order.shape[1], lax.axis_size("res"), term_counts.shape[0])
    rows, slabs, length = shape.rows, shape.slabs, shape.length
    f32 = jnp.float32
    vmem = pl.BlockSpec(memory_space=pltpu.VMEM)
    main_shape = (shape.chunks, slabs, shape.block, LANES)
    edge_shape = (slabs, TILE, LANES)
    table = fourier_table(rows)
    main, edge = pl.pallas_call(
        functools.partial(zeta_kernel, shape),
        out_shape=(jax.ShapeDtypeStruct(main_shape, f32), jax.ShapeDtypeStruct(edge_shape, f32)),
        in_specs=[pl.BlockSpec(memory_space=pltpu.SMEM), vmem, vmem, pl.BlockSpec(memory_space=pltpu.HBM)],
        out_specs=(vmem, vmem),
        scratch_shapes=[
            pltpu.VMEM(main_shape, f32),
            pltpu.VMEM(edge_shape, f32),
            pltpu.VMEM((1, length), jnp.int32),
            pltpu.VMEM((1, rows), jnp.int32),
            pltpu.VMEM((length, LANES), f32),
            pltpu.VMEM(table.shape, jnp.bfloat16),
            pltpu.VMEM((MAXN, TILE, rows), f32),
            pltpu.VMEM((MAXN, TILE, rows), f32),
            pltpu.VMEM((MAXN, TILE, rows), f32),
            pltpu.VMEM((MAXN, TILE, rows), f32),
            pltpu.VMEM((length + TILE, rows), f32),
            pltpu.VMEM((length + TILE, rows), f32),
            pltpu.VMEM((length + TILE, LANES), f32),
            pltpu.VMEM((rows, LANES), f32),
            pltpu.VMEM((rows, LANES), f32),
            pltpu.SemaphoreType.DMA,
            pltpu.SemaphoreType.DMA((4,)),
            pltpu.SemaphoreType.DMA((shape.chunks, slabs)),
            pltpu.SemaphoreType.DMA((shape.chunks, slabs)),
            pltpu.SemaphoreType.DMA((slabs,)),
            pltpu.SemaphoreType.DMA((slabs,)),
        ],
        compiler_params=pltpu.CompilerParams(
            collective_id=0, has_side_effects=True, vmem_limit_bytes=48 * 2**20
        ),
    )(t_start, log_order, term_counts[None, :], jnp.asarray(table))
    return refine_call(shape, main, edge)


def refine_call(shape, main, edge):
    slabs, length = shape.slabs, shape.length
    chunk = 16
    f32 = jnp.float32
    return pl.pallas_call(
        functools.partial(refine_kernel, shape, chunk),
        grid=(shape.block // chunk,),
        out_shape=jax.ShapeDtypeStruct((2, slabs, shape.block, 2 * length), f32),
        in_specs=[
            pl.BlockSpec((shape.chunks, slabs, chunk, LANES), lambda i: (0, 0, i, 0)),
            pl.BlockSpec((slabs, TILE, LANES), lambda i: (0, 0, 0)),
            pl.BlockSpec((2, length, 2 * length), lambda i: (0, 0, 0)),
            pl.BlockSpec((2, 2, slabs * TILE, slabs * LANES), lambda i: (0, 0, 0, 0)),
        ],
        out_specs=pl.BlockSpec((2, slabs, chunk, 2 * length), lambda i: (0, 0, i, 0)),
        scratch_shapes=[pltpu.VMEM((LANES, slabs * LANES), f32)],
        compiler_params=pltpu.CompilerParams(vmem_limit_bytes=48 * 2**20),
    )(main, edge, jnp.asarray(refine_table(length)), jnp.asarray(edge_table(length, slabs)))


time_step = 0.0625


def padded_2(block, sides, width):
    for axis, dim in sides:
        count = lax.axis_size(axis)
        forward = [(i, i + 1) for i in range(count - 1)]
        backward = [(target, source) for source, target in forward]
        low = lax.ppermute(
            lax.slice_in_dim(block, block.shape[dim] - width, None, axis=dim), axis, forward
        )
        high = lax.ppermute(lax.slice_in_dim(block, 0, width, axis=dim), axis, backward)
        block = jnp.concatenate([low, block, high], axis=dim)
    return block


def inverse_power(base_value, t_values):
    modulus = lax.rsqrt(base_value)
    phase_now = t_values * jnp.log(base_value)
    return (modulus * jnp.cos(phase_now), -modulus * jnp.sin(phase_now))


def hurwitz_values(x_values, t_values, count_row, most_terms):
    shape_out = (x_values.shape[0], t_values.shape[1])

    def add_term(term_index, running):
        sum_re, sum_im = running
        base_value = term_index.astype(x_values.dtype) + x_values
        piece_re, piece_im = inverse_power(base_value, t_values)
        active = term_index < count_row
        return (
            sum_re + jnp.where(active, piece_re, 0.0),
            sum_im + jnp.where(active, piece_im, 0.0),
        )

    zeros_init = jnp.zeros(shape_out, x_values.dtype)
    sum_re, sum_im = lax.fori_loop(0, most_terms, add_term, (zeros_init, zeros_init))
    tail_base = count_row.astype(x_values.dtype) + x_values
    power_re, power_im = inverse_power(tail_base, t_values)
    denominator = 0.25 + t_values * t_values
    lifted_re = tail_base * power_re
    lifted_im = tail_base * power_im
    total_re = sum_re + (-0.5 * lifted_re + t_values * lifted_im) / denominator + 0.5 * power_re
    total_im = sum_im + (-t_values * lifted_re - 0.5 * lifted_im) / denominator + 0.5 * power_im
    total_re = total_re + (0.5 * power_re - t_values * power_im) / (12.0 * tail_base)
    total_im = total_im + (0.5 * power_im + t_values * power_re) / (12.0 * tail_base)
    cubic_re = 1.875 - 4.5 * t_values * t_values
    cubic_im = 5.75 * t_values - t_values * t_values * t_values
    cube_base = 720.0 * tail_base * tail_base * tail_base
    total_re = total_re - (cubic_re * power_re - cubic_im * power_im) / cube_base
    total_im = total_im - (cubic_re * power_im + cubic_im * power_re) / cube_base
    return (total_re, total_im)


def refine(padded, half_width, length):
    coarse = padded[..., half_width : half_width + length]
    middle = jnp.zeros_like(coarse)
    for offset in range(1 - half_width, half_width + 1):
        weight = sinc_value(offset - 0.5) * sinc_value((offset - 0.5) / half_width)
        middle = middle + weight * padded[..., half_width + offset : half_width + offset + length]
    stacked = jnp.stack([coarse, middle], axis=-1)
    return stacked.reshape(stacked.shape[:-2] + (2 * length,))


def matmul_high(left, right):
    return jnp.dot(left, right, precision=lax.Precision.HIGHEST, preferred_element_type=jnp.float32)


def per_device(log_order, t_start, term_counts):
    rows_here = log_order.shape[1]
    slabs = lax.axis_size("res")
    slab_index = lax.axis_index("res")
    length_here = term_counts.shape[0]
    ta_index = lax.axis_index("ta")
    modulus_int = slabs * rows_here + 1
    x_values = log_order.reshape(rows_here, 1).astype(jnp.float32) / jnp.float32(modulus_int)
    row_ids = jnp.arange(rows_here, dtype=jnp.int32)
    first_phase = (row_ids[:, None] * row_ids[None, :] % rows_here).astype(jnp.float32) * (
        2.0 * math.pi / rows_here
    )
    first_cos = jnp.cos(first_phase)
    first_sin = jnp.sin(first_phase)
    twist_phase = (row_ids * slab_index).astype(jnp.float32)[:, None] * (
        2.0 * math.pi / (slabs * rows_here)
    )
    twist_cos = jnp.cos(twist_phase)
    twist_sin = jnp.sin(twist_phase)
    slab_ids = jnp.arange(slabs, dtype=jnp.int32)
    second_phase = (slab_ids[:, None] * slab_ids[None, :] % slabs).astype(jnp.float32) * (
        2.0 * math.pi / slabs
    )
    second_cos = jnp.cos(second_phase)
    second_sin = jnp.sin(second_phase)
    positions = ta_index * length_here + jnp.arange(length_here, dtype=jnp.int32)
    count_row = term_counts[None, :]
    t_values = ((t_start[0] + positions).astype(jnp.float32) * time_step)[None, :]
    zeta_re, zeta_im = hurwitz_values(x_values, t_values, count_row, MAXN)
    mixed_re = matmul_high(first_cos, zeta_re) - matmul_high(first_sin, zeta_im)
    mixed_im = matmul_high(first_sin, zeta_re) + matmul_high(first_cos, zeta_im)
    turned_re = twist_cos * mixed_re - twist_sin * mixed_im
    turned_im = twist_sin * mixed_re + twist_cos * mixed_im
    sectioned = jnp.stack([turned_re, turned_im])[:, None]
    block_in = lax.all_to_all(sectioned, "res", split_axis=2, concat_axis=1, tiled=True)
    part_re = block_in[0]
    part_im = block_in[1]

    def mix(table, values):
        return jnp.einsum(
            "wp,psn->wsn",
            table,
            values,
            precision=lax.Precision.HIGHEST,
            preferred_element_type=jnp.float32,
        )

    out_re = mix(second_cos, part_re) - mix(second_sin, part_im)
    out_im = mix(second_sin, part_re) + mix(second_cos, part_im)
    spectrum = jnp.stack([out_re, out_im])
    factor_re, factor_im = inverse_power(jnp.float32(modulus_int), t_values)
    lval_re = spectrum[0] * factor_re - spectrum[1] * factor_im
    lval_im = spectrum[0] * factor_im + spectrum[1] * factor_re
    lvals = jnp.stack([lval_re, lval_im])
    padded = padded_2(lvals, (("ta", 3),), TAPS)
    return refine(padded, TAPS, length_here)


def solution(mesh):
    placed = (P("res", None), P("grp"), P(("grp", "ta")))
    return jax.shard_map(
        fast_device if mesh.shape["res"] == 8 and mesh.shape["ta"] == 2 else per_device,
        mesh=mesh,
        in_specs=placed,
        out_specs=P(None, None, "res", ("grp", "ta")),
        check_vma=False,
    )
```

```python
import functools
import math

import jax
import jax.numpy as jnp
import ml_dtypes
import numpy as np
from jax import lax
from jax.experimental import pallas as pl
from jax.experimental.pallas import tpu as pltpu
from jax.sharding import PartitionSpec as P

TAPS = 8
MAXN = 32
NMIN = 4
LANES = 128
HALF = LANES // 2
PEER_ORDER = (6, 7, 4, 5, 2, 3, 1)
NEAR_ORDER = (2, 3, 1)
TWICE = 2
TILE = 8

SIN_COEFS = (
    6.2831854820251465, -41.34170150756836, 81.60513305664062, -76.7030029296875,
    42.02585220336914, -14.899578094482422, 3.2377800941467285,
)
COS_COEFS = (
    1.0, -19.73920440673828, 64.93911743164062, -85.45011138916016,
    60.16743087768555, -25.96688461303711, 6.527706146240234,
)
ROUNDER = 12582912.0


def sincos_turns(turns):
    frac = turns - ((turns + ROUNDER) - ROUNDER)
    square = frac * frac
    sin_acc = jnp.full_like(square, SIN_COEFS[-1])
    cos_acc = jnp.full_like(square, COS_COEFS[-1])
    for sin_c, cos_c in zip(SIN_COEFS[-2::-1], COS_COEFS[-2::-1]):
        sin_acc = sin_acc * square + sin_c
        cos_acc = cos_acc * square + cos_c
    return sin_acc * frac, cos_acc


def split_bf16(values):
    high = values.astype(jnp.bfloat16)
    return high, (values - high.astype(jnp.float32)).astype(jnp.bfloat16)


def split_const(values):
    high = values.astype(np.float32).astype(ml_dtypes.bfloat16)
    low = (values - high.astype(np.float64)).astype(np.float32).astype(ml_dtypes.bfloat16)
    return high, low


def dot_nt(left, right):
    return lax.dot_general(
        left, right, (((1,), (1,)), ((), ())), preferred_element_type=jnp.float32
    )


def dot_nn(left, right):
    return jnp.dot(left, right, preferred_element_type=jnp.float32)


def fourier_table(rows):
    ids = np.arange(rows)
    phase = 2.0 * np.pi * (np.outer(ids, ids) % rows) / rows
    return np.stack(split_const(np.cos(phase)) + split_const(np.sin(phase)))


def sinc_value(offset):
    return math.sin(math.pi * offset) / (math.pi * offset)


def tap_weight(offset):
    return sinc_value(offset - 0.5) * sinc_value((offset - 0.5) / TAPS)


def refine_table(length):
    table = np.zeros((length, 2 * length))
    for m in range(length):
        table[m, 2 * m] = 1.0
        for offset in range(1 - TAPS, TAPS + 1):
            if 0 <= m + offset < length:
                table[m + offset, 2 * m + 1] = tap_weight(offset)
    return np.stack(split_const(table))


def edge_table(length, slabs):
    side = np.zeros((2, TILE, LANES))
    for h in range(TAPS):
        for column in range(LANES):
            if column % 2 == 0:
                continue
            m = (2 * length - LANES + column) // 2
            offset = length + h - m
            if 1 - TAPS <= offset <= TAPS:
                side[0, h, column] = tap_weight(offset)
            m = column // 2
            offset = h - TAPS - m
            if 1 - TAPS <= offset <= TAPS:
                side[1, h, column] = tap_weight(offset)
    full = np.zeros((2, slabs * TILE, slabs * LANES))
    for slab in range(slabs):
        full[:, slab * TILE : (slab + 1) * TILE, slab * LANES : (slab + 1) * LANES] = side
    high, low = split_const(full)
    return np.stack([high, low], axis=1)


class Shape:
    def __init__(self, rows, slabs, length):
        self.rows = rows
        self.slabs = slabs
        self.length = length
        self.block = rows // slabs
        self.tiles = length // TILE + 1
        self.halves = length // LANES
        self.chunks = length // HALF


def prepare(shape, order_ref, turn_re, turn_im, wave_re, wave_im, base_t):
    rows = shape.rows
    modulus = float(shape.slabs * rows + 1)
    order_row = order_ref[...].astype(jnp.float32)
    term = lax.broadcasted_iota(jnp.int32, (MAXN, rows), 0).astype(jnp.float32)
    base = term * modulus + order_row
    log_turn = jnp.log(base) * (1.0 / (2.0 * math.pi))
    amp = lax.rsqrt(base)
    step_sin, step_cos = sincos_turns(log_turn * (TILE / 16.0))
    offsets = lax.broadcasted_iota(jnp.int32, (TILE, rows), 0).astype(jnp.float32)
    t_first = (base_t + offsets) * 0.0625
    for n in range(MAXN):
        sin, cos = sincos_turns(t_first * log_turn[n : n + 1, :])
        amp_row = amp[n : n + 1, :]
        wave_re[n] = amp_row * cos
        wave_im[n] = -amp_row * sin
        turn_re[n] = jnp.broadcast_to(step_cos[n : n + 1, :], (TILE, rows))
        turn_im[n] = jnp.broadcast_to(-step_sin[n : n + 1, :], (TILE, rows))


def sum_tiles(shape, first, count, order_ref, counts, turn_re, turn_im, wave_re, wave_im, zeta_re, zeta_im, base_t):
    modulus = float(shape.slabs * shape.rows + 1)
    row0 = first * TILE
    offsets = lax.broadcasted_iota(jnp.int32, (TILE, LANES), 0).astype(jnp.float32)
    per_tile = []
    for a in range(count):
        t_now = (base_t + float(row0 + a * TILE) + offsets) * 0.0625
        t_square = t_now * t_now
        per_tile.append((t_now, 1.0 / (0.25 + t_square), 1.875 - 4.5 * t_square, t_now * (5.75 - t_square)))

    def lane_block(block, carry):
        lanes = pl.ds(pl.multiple_of(block * LANES, LANES), LANES)
        limits = [counts[row0 + a * TILE : row0 + (a + 1) * TILE, :] for a in range(count)]

        def term(n, sums, masked):
            now_re = wave_re[n, :, lanes]
            now_im = wave_im[n, :, lanes]
            rot_re = turn_re[n, :, lanes]
            rot_im = turn_im[n, :, lanes]
            twice_cos = rot_re + rot_re
            last_re = last_im = None
            out = []
            for a in range(count):
                if masked:
                    active = limits[a] > lax.convert_element_type(n, jnp.float32)
                    out.append(sums[2 * a] + jnp.where(active, now_re, 0.0))
                    out.append(sums[2 * a + 1] + jnp.where(active, now_im, 0.0))
                else:
                    out.append(sums[2 * a] + now_re)
                    out.append(sums[2 * a + 1] + now_im)
                if a == 0:
                    next_re = now_re * rot_re - now_im * rot_im
                    next_im = now_re * rot_im + now_im * rot_re
                else:
                    next_re = twice_cos * now_re - last_re
                    next_im = twice_cos * now_im - last_im
                last_re, last_im, now_re, now_im = now_re, now_im, next_re, next_im
            wave_re[n, :, lanes] = now_re
            wave_im[n, :, lanes] = now_im
            return tuple(out)

        sums = (jnp.zeros((TILE, LANES), jnp.float32),) * (2 * count)
        for n in range(NMIN):
            sums = term(n, sums, False)
        sums = lax.fori_loop(NMIN, MAXN, functools.partial(term, masked=True), sums, unroll=4)
        residue = jnp.broadcast_to(order_ref[:, lanes].astype(jnp.float32), (TILE, LANES))
        fraction = residue * (1.0 / modulus)
        for a in range(count):
            limit = limits[a]
            t_now, inverse_den, cubic_re, cubic_im = per_tile[a]
            whole_base = limit * modulus + residue
            tail_base = limit + fraction
            inverse = 1.0 / tail_base
            cube = inverse * inverse * inverse * (1.0 / 720.0)
            twelfth = inverse * (1.0 / 12.0)
            lifted = tail_base * inverse_den
            gain_re = 0.5 + 0.5 * twelfth - 0.5 * lifted - cubic_re * cube
            gain_im = t_now * (twelfth - lifted) - cubic_im * cube
            sin, cos = sincos_turns(t_now * (jnp.log(whole_base) * (1.0 / (2.0 * math.pi))))
            amp = lax.rsqrt(whole_base)
            power_re = amp * cos
            power_im = -amp * sin
            place = slice(row0 + a * TILE, row0 + (a + 1) * TILE)
            zeta_re[place, lanes] = sums[2 * a] + (gain_re * power_re - gain_im * power_im)
            zeta_im[place, lanes] = sums[2 * a + 1] + (gain_re * power_im + gain_im * power_re)
        return carry

    lax.fori_loop(0, shape.rows // LANES, lane_block, 0)


def make_twist(shape, slab_index, twist_cos, twist_sin):
    ids = lax.broadcasted_iota(jnp.int32, (shape.rows, LANES), 0)
    turns = (ids * slab_index).astype(jnp.float32) * (1.0 / (shape.slabs * shape.rows))
    sin, cos = sincos_turns(turns)
    twist_cos[...] = cos
    twist_sin[...] = sin


def transform_chunk(shape, chunk, skip, first_block, blocks, zeta_re, zeta_im, tables, twist_cos, twist_sin, store):
    place = pl.ds(pl.multiple_of(chunk * HALF + skip, TILE), HALF)
    high, low = split_bf16(jnp.concatenate([zeta_re[place, :], zeta_im[place, :]], axis=0))
    both = jnp.concatenate([high, low], axis=0)
    cut_rows = 2 * shape.block
    lane = lax.broadcasted_iota(jnp.int32, (cut_rows, LANES), 1)
    sign = jnp.where(lane < HALF, -1.0, 1.0)
    for piece in range(blocks // 2):
        start = first_block * shape.block + piece * cut_rows
        rows = pl.ds(pl.multiple_of(start, cut_rows), cut_rows)
        with_cos = dot_nt(tables[0, rows, :], both)
        with_sin = dot_nt(tables[2, rows, :], both)
        with_cos = with_cos[:, :LANES] + with_cos[:, LANES:] + dot_nt(tables[1, rows, :], high)
        with_sin = with_sin[:, :LANES] + with_sin[:, LANES:] + dot_nt(tables[3, rows, :], high)
        mixed = with_cos + sign * pltpu.roll(with_sin, HALF, 1)
        out = twist_cos[rows, :] * mixed + (sign * twist_sin[rows, :]) * pltpu.roll(mixed, HALF, 1)
        for sub in range(2):
            store(2 * piece + sub, out[sub * shape.block : (sub + 1) * shape.block])


def transform_edge(shape, place, slab_index, zeta_re, zeta_im, tables, store):
    both = jnp.concatenate([zeta_re[place, :], zeta_im[place, :]], axis=0)
    high, low = split_bf16(both)
    with_cos = dot_nn(high, tables[0]) + dot_nn(low, tables[0]) + dot_nn(high, tables[1])
    with_sin = dot_nn(high, tables[2]) + dot_nn(low, tables[2]) + dot_nn(high, tables[3])
    mixed_re = with_cos[:TILE] - with_sin[TILE:]
    mixed_im = with_sin[:TILE] + with_cos[TILE:]
    ids = lax.broadcasted_iota(jnp.int32, (TILE, shape.rows), 1)
    sin, cos = sincos_turns(
        (ids * slab_index).astype(jnp.float32) * (1.0 / (shape.slabs * shape.rows))
    )
    out_re = cos * mixed_re - sin * mixed_im
    out_im = sin * mixed_re + cos * mixed_im
    lane = lax.broadcasted_iota(jnp.int32, (TILE, LANES), 1)
    for pair in range(shape.slabs // 2):
        cut = slice(pair * LANES, (pair + 1) * LANES)
        part_re = out_re[:, cut]
        part_im = out_im[:, cut]
        store(2 * pair, jnp.where(lane < LANES // 2, part_re, pltpu.roll(part_im, LANES // 2, 1)))
        store(
            2 * pair + 1,
            jnp.where(lane < LANES // 2, pltpu.roll(part_re, LANES // 2, 1), part_im),
        )


def column_counts(shape, own_row, other_row, own_at, other_from, other_at, counts, spare):
    def columns(row_ref, cut):
        lanes = slice(cut * LANES, (cut + 1) * LANES)
        return jnp.broadcast_to(row_ref[:, lanes].astype(jnp.float32), (LANES, LANES)).T

    for cut in range(shape.halves):
        at = pl.ds(pl.multiple_of(own_at + cut * LANES, TILE), LANES)
        counts[at, :] = columns(own_row, cut)
        spare[cut * LANES : (cut + 1) * LANES, :] = columns(other_row, cut)
    counts[pl.ds(pl.multiple_of(other_at, TILE), TILE), :] = spare[
        pl.ds(pl.multiple_of(other_from, TILE), TILE), :
    ]


def flipped(index, bits):
    for bit in (1, 2, 4):
        if bits & bit:
            index = index + bit * (1 - 2 * ((index // bit) % 2))
    return index


def zeta_kernel(shape, start_ref, order_ref, count_ref, table_hbm, main_out, edge_out, main_send, edge_send,
                other_counts, other_order, spare, tables, turn_re, turn_im, wave_re, wave_im, zeta_re, zeta_im, counts,
                twist_cos, twist_sin, table_sem, count_sems, main_send_sems, main_recv_sems,
                edge_send_sems, edge_recv_sems):
    slabs, length = shape.slabs, shape.length
    me = lax.axis_index("res")
    ta_index = lax.axis_index("ta")
    mesh_ids = pl.DeviceIdType.MESH
    peers = [flipped(me, d) for d in range(slabs)]

    barrier = pltpu.get_barrier_semaphore()
    for d in range(1, slabs):
        pl.semaphore_signal(barrier, inc=1, device_id={"res": peers[d]}, device_id_type=mesh_ids)
    pl.semaphore_signal(barrier, inc=1, device_id={"ta": 1 - ta_index}, device_id_type=mesh_ids)
    table_copy = pltpu.make_async_copy(table_hbm, tables, table_sem)
    table_copy.start()

    base_t = (start_ref[0] + ta_index * (length - TILE)).astype(jnp.float32)
    make_twist(shape, me, twist_cos, twist_sin)
    pl.semaphore_wait(barrier, slabs)
    count_copy = pltpu.make_async_remote_copy(
        src_ref=count_ref, dst_ref=other_counts, send_sem=count_sems.at[0], recv_sem=count_sems.at[1],
        device_id={"ta": 1 - ta_index}, device_id_type=mesh_ids,
    )
    count_copy.start()
    order_copy = pltpu.make_async_remote_copy(
        src_ref=order_ref, dst_ref=other_order, send_sem=count_sems.at[2], recv_sem=count_sems.at[3],
        device_id={"res": peers[slabs // 2]}, device_id_type=mesh_ids,
    )
    order_copy.start()
    prepare(shape, order_ref, turn_re, turn_im, wave_re, wave_im, base_t)
    count_copy.wait()
    order_copy.wait()
    column_counts(shape, count_ref, other_counts, ta_index * TILE, ta_index * (length - TILE),
                  (1 - ta_index) * length, counts, spare)

    copies = []

    def send(source, target, send_sems, recv_sems, d):
        copy = pltpu.make_async_remote_copy(
            src_ref=source, dst_ref=target, send_sem=send_sems, recv_sem=recv_sems,
            device_id={"res": peers[d]}, device_id_type=mesh_ids,
        )
        copy.start()
        copies.append(copy)

    def sums_and_blocks(order, chunk, extra, first, blocks, store):
        start = chunk * (HALF // TILE) + (0 if extra else 1)
        sum_tiles(shape, start, HALF // TILE + extra, order, counts, turn_re, turn_im, wave_re, wave_im,
                  zeta_re, zeta_im, base_t)
        if order is order_ref and chunk == 0:
            table_copy.wait()
        transform_chunk(shape, chunk, ta_index * TILE, first, blocks, zeta_re, zeta_im, tables,
                        twist_cos, twist_sin, store)

    near = slabs // 2
    near_first = (me // near) * near
    far_first = near - near_first
    split = shape.chunks - TWICE
    for chunk in range(shape.chunks):
        wide = chunk < split
        first = 0 if wide else near_first

        def store(block, values, chunk=chunk, first=first):
            main_send[chunk, first + block] = values

        sums_and_blocks(order_ref, chunk, int(chunk == 0), first, slabs if wide else near, store)
        for d in PEER_ORDER if wide else NEAR_ORDER:
            send(main_send.at[chunk, peers[d]], main_out.at[chunk, me],
                 main_send_sems.at[chunk, d], main_recv_sems.at[chunk, d], d)
        main_out[chunk, me] = main_send[chunk, me]

    def store_edge(block, values):
        edge_send[block] = values

    edge_place = pl.ds(pl.multiple_of((1 - ta_index) * length, TILE), TILE)
    transform_edge(shape, edge_place, me, zeta_re, zeta_im, tables, store_edge)
    for d in PEER_ORDER:
        send(edge_send.at[peers[d]], edge_out.at[me], edge_send_sems.at[d], edge_recv_sems.at[d], d)
    edge_out[me] = edge_send[me]

    partner = peers[near]
    prepare(shape, other_order, turn_re, turn_im, wave_re, wave_im, base_t + float(split * HALF))
    make_twist(shape, partner, twist_cos, twist_sin)
    for chunk in range(split, shape.chunks):

        def store(block, values, chunk=chunk):
            main_send[chunk, far_first + block] = values

        sums_and_blocks(other_order, chunk, int(chunk == split), near_first, near, store)
        for d in NEAR_ORDER:
            send(main_send.at[chunk, peers[near + d]], main_out.at[chunk, partner],
                 main_send_sems.at[chunk, near + d], main_recv_sems.at[chunk, near + d], d)
        main_out[chunk, partner] = main_send[chunk, partner]
    for copy in copies:
        copy.wait()


def turn_eighth(re, im, eighths):
    root = math.sqrt(0.5)
    if eighths == 0:
        return re, im
    if eighths == 1:
        return root * (re - im), root * (re + im)
    if eighths == 2:
        return -im, re
    return -root * (re + im), root * (re - im)


def fft_eight(parts):
    def step(values):
        size = len(values)
        if size == 1:
            return values
        even = step(values[0::2])
        odd = step(values[1::2])
        low, high = [], []
        for k in range(size // 2):
            o_re, o_im = turn_eighth(*odd[k], k * (8 // size))
            e_re, e_im = even[k]
            low.append((e_re + o_re, e_im + o_im))
            high.append((e_re - o_re, e_im - o_im))
        return low + high

    return step(parts)


def refine_kernel(shape, chunk, main_ref, edge_ref, table, edge_tab, out_ref, edge_out):
    step = pl.program_id(0)
    slabs = shape.slabs
    half_lanes = LANES // 2
    ta_index = lax.axis_index("ta")

    @pl.when(step == 0)
    def _():
        lane = lax.broadcasted_iota(jnp.int32, (TILE, LANES), 1)
        parts = [(edge_ref[p], pltpu.roll(edge_ref[p], half_lanes, 1)) for p in range(slabs)]
        mixed = fft_eight(parts)
        rows = [jnp.where(lane < half_lanes, re, pltpu.roll(im, half_lanes, 1)) for re, im in mixed]
        stacked = jnp.concatenate(rows + rows, axis=0)
        high, low = split_bf16(stacked.T[:, : slabs * TILE])
        tab_high = edge_tab[ta_index, 0]
        tab_low = edge_tab[ta_index, 1]
        edge_out[...] = dot_nn(high, tab_high) + dot_nn(low, tab_high) + dot_nn(high, tab_low)

    low_half = lax.broadcasted_iota(jnp.int32, (chunk, LANES), 1) < half_lanes
    parts = []
    for p in range(slabs):
        re, im = [], []
        for h in range(shape.halves):
            left = main_ref[2 * h, p]
            right = main_ref[2 * h + 1, p]
            re.append(jnp.where(low_half, left, pltpu.roll(right, half_lanes, 1)))
            im.append(jnp.where(low_half, pltpu.roll(left, half_lanes, 1), right))
        parts.append((jnp.concatenate(re, axis=1), jnp.concatenate(im, axis=1)))
    mixed = fft_eight(parts)
    stacked = jnp.concatenate([m[0] for m in mixed] + [m[1] for m in mixed], axis=0)
    high, low = split_bf16(stacked)
    result = dot_nn(high, table[0]) + dot_nn(low, table[0]) + dot_nn(high, table[1])
    edge_lanes = pl.ds(
        pl.multiple_of((1 - ta_index) * (2 * shape.length - LANES), LANES), LANES
    )
    for part in range(2):
        rows = pl.ds(pl.multiple_of(part * shape.block + step * chunk, TILE), chunk)
        for w in range(slabs):
            at = (part * slabs + w) * chunk
            out_ref[part, w] = result[at : at + chunk]
            out_ref[part, w, :, edge_lanes] += edge_out[rows, w * LANES : (w + 1) * LANES]


def fast_device(log_order, t_start, term_counts):
    shape = Shape(log_order.shape[1], lax.axis_size("res"), term_counts.shape[0])
    rows, slabs, length = shape.rows, shape.slabs, shape.length
    f32 = jnp.float32
    vmem = pl.BlockSpec(memory_space=pltpu.VMEM)
    main_shape = (shape.chunks, slabs, shape.block, LANES)
    edge_shape = (slabs, TILE, LANES)
    table = fourier_table(rows)
    main, edge = pl.pallas_call(
        functools.partial(zeta_kernel, shape),
        out_shape=(jax.ShapeDtypeStruct(main_shape, f32), jax.ShapeDtypeStruct(edge_shape, f32)),
        in_specs=[pl.BlockSpec(memory_space=pltpu.SMEM), vmem, vmem, pl.BlockSpec(memory_space=pltpu.HBM)],
        out_specs=(vmem, vmem),
        scratch_shapes=[
            pltpu.VMEM(main_shape, f32),
            pltpu.VMEM(edge_shape, f32),
            pltpu.VMEM((1, length), jnp.int32),
            pltpu.VMEM((1, rows), jnp.int32),
            pltpu.VMEM((length, LANES), f32),
            pltpu.VMEM(table.shape, jnp.bfloat16),
            pltpu.VMEM((MAXN, TILE, rows), f32),
            pltpu.VMEM((MAXN, TILE, rows), f32),
            pltpu.VMEM((MAXN, TILE, rows), f32),
            pltpu.VMEM((MAXN, TILE, rows), f32),
            pltpu.VMEM((length + TILE, rows), f32),
            pltpu.VMEM((length + TILE, rows), f32),
            pltpu.VMEM((length + TILE, LANES), f32),
            pltpu.VMEM((rows, LANES), f32),
            pltpu.VMEM((rows, LANES), f32),
            pltpu.SemaphoreType.DMA,
            pltpu.SemaphoreType.DMA((4,)),
            pltpu.SemaphoreType.DMA((shape.chunks, slabs)),
            pltpu.SemaphoreType.DMA((shape.chunks, slabs)),
            pltpu.SemaphoreType.DMA((slabs,)),
            pltpu.SemaphoreType.DMA((slabs,)),
        ],
        compiler_params=pltpu.CompilerParams(
            collective_id=0, has_side_effects=True, vmem_limit_bytes=48 * 2**20
        ),
    )(t_start, log_order, term_counts[None, :], jnp.asarray(table))
    return refine_call(shape, main, edge)


def refine_call(shape, main, edge):
    slabs, length = shape.slabs, shape.length
    chunk = 16
    f32 = jnp.float32
    return pl.pallas_call(
        functools.partial(refine_kernel, shape, chunk),
        grid=(shape.block // chunk,),
        out_shape=jax.ShapeDtypeStruct((2, slabs, shape.block, 2 * length), f32),
        in_specs=[
            pl.BlockSpec((shape.chunks, slabs, chunk, LANES), lambda i: (0, 0, i, 0)),
            pl.BlockSpec((slabs, TILE, LANES), lambda i: (0, 0, 0)),
            pl.BlockSpec((2, length, 2 * length), lambda i: (0, 0, 0)),
            pl.BlockSpec((2, 2, slabs * TILE, slabs * LANES), lambda i: (0, 0, 0, 0)),
        ],
        out_specs=pl.BlockSpec((2, slabs, chunk, 2 * length), lambda i: (0, 0, i, 0)),
        scratch_shapes=[pltpu.VMEM((LANES, slabs * LANES), f32)],
        compiler_params=pltpu.CompilerParams(vmem_limit_bytes=48 * 2**20),
    )(main, edge, jnp.asarray(refine_table(length)), jnp.asarray(edge_table(length, slabs)))


time_step = 0.0625


def padded_2(block, sides, width):
    for axis, dim in sides:
        count = lax.axis_size(axis)
        forward = [(i, i + 1) for i in range(count - 1)]
        backward = [(target, source) for source, target in forward]
        low = lax.ppermute(
            lax.slice_in_dim(block, block.shape[dim] - width, None, axis=dim), axis, forward
        )
        high = lax.ppermute(lax.slice_in_dim(block, 0, width, axis=dim), axis, backward)
        block = jnp.concatenate([low, block, high], axis=dim)
    return block


def inverse_power(base_value, t_values):
    modulus = lax.rsqrt(base_value)
    phase_now = t_values * jnp.log(base_value)
    return (modulus * jnp.cos(phase_now), -modulus * jnp.sin(phase_now))


def hurwitz_values(x_values, t_values, count_row, most_terms):
    shape_out = (x_values.shape[0], t_values.shape[1])

    def add_term(term_index, running):
        sum_re, sum_im = running
        base_value = term_index.astype(x_values.dtype) + x_values
        piece_re, piece_im = inverse_power(base_value, t_values)
        active = term_index < count_row
        return (
            sum_re + jnp.where(active, piece_re, 0.0),
            sum_im + jnp.where(active, piece_im, 0.0),
        )

    zeros_init = jnp.zeros(shape_out, x_values.dtype)
    sum_re, sum_im = lax.fori_loop(0, most_terms, add_term, (zeros_init, zeros_init))
    tail_base = count_row.astype(x_values.dtype) + x_values
    power_re, power_im = inverse_power(tail_base, t_values)
    denominator = 0.25 + t_values * t_values
    lifted_re = tail_base * power_re
    lifted_im = tail_base * power_im
    total_re = sum_re + (-0.5 * lifted_re + t_values * lifted_im) / denominator + 0.5 * power_re
    total_im = sum_im + (-t_values * lifted_re - 0.5 * lifted_im) / denominator + 0.5 * power_im
    total_re = total_re + (0.5 * power_re - t_values * power_im) / (12.0 * tail_base)
    total_im = total_im + (0.5 * power_im + t_values * power_re) / (12.0 * tail_base)
    cubic_re = 1.875 - 4.5 * t_values * t_values
    cubic_im = 5.75 * t_values - t_values * t_values * t_values
    cube_base = 720.0 * tail_base * tail_base * tail_base
    total_re = total_re - (cubic_re * power_re - cubic_im * power_im) / cube_base
    total_im = total_im - (cubic_re * power_im + cubic_im * power_re) / cube_base
    return (total_re, total_im)


def refine(padded, half_width, length):
    coarse = padded[..., half_width : half_width + length]
    middle = jnp.zeros_like(coarse)
    for offset in range(1 - half_width, half_width + 1):
        weight = sinc_value(offset - 0.5) * sinc_value((offset - 0.5) / half_width)
        middle = middle + weight * padded[..., half_width + offset : half_width + offset + length]
    stacked = jnp.stack([coarse, middle], axis=-1)
    return stacked.reshape(stacked.shape[:-2] + (2 * length,))


def matmul_high(left, right):
    return jnp.dot(left, right, precision=lax.Precision.HIGHEST, preferred_element_type=jnp.float32)


def per_device(log_order, t_start, term_counts):
    rows_here = log_order.shape[1]
    slabs = lax.axis_size("res")
    slab_index = lax.axis_index("res")
    length_here = term_counts.shape[0]
    ta_index = lax.axis_index("ta")
    modulus_int = slabs * rows_here + 1
    x_values = log_order.reshape(rows_here, 1).astype(jnp.float32) / jnp.float32(modulus_int)
    row_ids = jnp.arange(rows_here, dtype=jnp.int32)
    first_phase = (row_ids[:, None] * row_ids[None, :] % rows_here).astype(jnp.float32) * (
        2.0 * math.pi / rows_here
    )
    first_cos = jnp.cos(first_phase)
    first_sin = jnp.sin(first_phase)
    twist_phase = (row_ids * slab_index).astype(jnp.float32)[:, None] * (
        2.0 * math.pi / (slabs * rows_here)
    )
    twist_cos = jnp.cos(twist_phase)
    twist_sin = jnp.sin(twist_phase)
    slab_ids = jnp.arange(slabs, dtype=jnp.int32)
    second_phase = (slab_ids[:, None] * slab_ids[None, :] % slabs).astype(jnp.float32) * (
        2.0 * math.pi / slabs
    )
    second_cos = jnp.cos(second_phase)
    second_sin = jnp.sin(second_phase)
    positions = ta_index * length_here + jnp.arange(length_here, dtype=jnp.int32)
    count_row = term_counts[None, :]
    t_values = ((t_start[0] + positions).astype(jnp.float32) * time_step)[None, :]
    zeta_re, zeta_im = hurwitz_values(x_values, t_values, count_row, MAXN)
    mixed_re = matmul_high(first_cos, zeta_re) - matmul_high(first_sin, zeta_im)
    mixed_im = matmul_high(first_sin, zeta_re) + matmul_high(first_cos, zeta_im)
    turned_re = twist_cos * mixed_re - twist_sin * mixed_im
    turned_im = twist_sin * mixed_re + twist_cos * mixed_im
    sectioned = jnp.stack([turned_re, turned_im])[:, None]
    block_in = lax.all_to_all(sectioned, "res", split_axis=2, concat_axis=1, tiled=True)
    part_re = block_in[0]
    part_im = block_in[1]

    def mix(table, values):
        return jnp.einsum(
            "wp,psn->wsn",
            table,
            values,
            precision=lax.Precision.HIGHEST,
            preferred_element_type=jnp.float32,
        )

    out_re = mix(second_cos, part_re) - mix(second_sin, part_im)
    out_im = mix(second_sin, part_re) + mix(second_cos, part_im)
    spectrum = jnp.stack([out_re, out_im])
    factor_re, factor_im = inverse_power(jnp.float32(modulus_int), t_values)
    lval_re = spectrum[0] * factor_re - spectrum[1] * factor_im
    lval_im = spectrum[0] * factor_im + spectrum[1] * factor_re
    lvals = jnp.stack([lval_re, lval_im])
    padded = padded_2(lvals, (("ta", 3),), TAPS)
    return refine(padded, TAPS, length_here)


def solution(mesh):
    placed = (P("res", None), P("grp"), P(("grp", "ta")))
    return jax.shard_map(
        fast_device if mesh.shape["res"] == 8 and mesh.shape["ta"] == 2 else per_device,
        mesh=mesh,
        in_specs=placed,
        out_specs=P(None, None, "res", ("grp", "ta")),
        check_vma=False,
    )
```
